32 devices in a mesh: tile: 8 (over z, core), dp: 4 (over y, x).
Axes of the slice: x: 2, y: 2, z: 4, core: 2. Of those that a mesh axis runs over, the one named last changes fastest.
Arguments:
- clip_frames: bfloat16 [4, 8, 32, 8, 128], P('dp', None, 'tile'), may hold values from -6 to 6
- segments: int32 [4, 8], P('dp'), may hold values from 0 to 2, never falling along the last dimension, each value on 1 to 4 neighbouring positions
- weight_first: bfloat16 [3456, 128], replicated, may hold values from -0.109375 to 0.109375
- weight_second: bfloat16 [3456, 128], replicated, may hold values from -0.109375 to 0.109375
- cotangent: bfloat16 [4, 8, 16, 4, 128], P('dp', None, 'tile'), may hold values from -6 to 6
Outputs:
- pooled: float32 [4, 8, 16, 4, 128], P('dp', None, 'tile')
- input_grad: float32 [4, 8, 32, 8, 128], P('dp', None, 'tile')
- grad_first: float32 [3456, 128], P('tile')
- grad_second: float32 [3456, 128], P('tile')
The draws below stay inside these ranges and needn't reach their ends.
Inputs may be any that keep to these rules, and one draw needn't show every extreme that they name: `segments`: clip numbers never fall along the frames of a sequence; each clip is one to 4 frames long and one clip has exactly 4.
All inputs are finite; a program needn't handle non-finite values.
Results may differ from the reference program's by a relative error of at most 0.0029.
Values may be sent and summed in bfloat16 or wider, within the bound.
A program may use at most 64 MiB of HBM per device.

```python
import math
import jax
import jax.numpy as jnp
import numpy as np
from jax import lax

C = 128
FRAMES = 8
WW = 8
GROUPS = 4
H = 32


def block_scale(stream_key, extent, cuts, low, top_value):
    level = 1.0
    for dim, shards_of in cuts:
        heights = jax.random.uniform(jax.random.fold_in(jax.random.fold_in(stream_key, 6), dim), (shards_of,), jnp.float32, low / len(cuts), top_value / len(cuts))
        level = level * jnp.repeat(jnp.exp(heights), extent[dim] // shards_of).reshape((-1,) + (1,) * (len(extent) - 1 - dim))
    return level


def profile(amount, total, bound, skew):
    loads = [(1 << 20) // math.isqrt(grade ** skew) + 1 for grade in range(2, amount + 1)]
    rest, given = total - bound - (amount - 1), [1] * (amount - 1)
    while rest > 0:
        free = [i for i in range(amount - 1) if given[i] < bound]
        whole, budget = sum([loads[i] for i in free]), rest
        for i in free:
            more = min(bound - given[i], max(1, budget * loads[i] // whole), rest)
            given[i] = given[i] + more
            rest = rest - more
    return np.array([bound] + given)


def ragged(stream_key, number_of, total, most, skew):
    if number_of == 2:
        one = jax.random.randint(stream_key, (), max(1, total - most), min(most, total - 1) + 1)
        return jnp.stack([one, total - one])
    tallies = jnp.asarray(profile(number_of, total, most, skew), jnp.int32)
    pairs = (number_of - 1) // 2
    giver, taker = tallies[1:1 + 2 * pairs:2], tallies[2:2 + 2 * pairs:2]
    margin = jnp.minimum(giver - 1, most - taker)
    moved = jax.random.randint(jax.random.fold_in(stream_key, 1), (pairs,), 0, 1 << 20) % (margin + 1)
    tallies = tallies.at[1:1 + 2 * pairs:2].set(giver - moved).at[2:2 + 2 * pairs:2].set(taker + moved)
    return tallies[jax.random.permutation(jax.random.fold_in(stream_key, 2), number_of)]


def centred(stream_key, extent, spread, limit, cuts=(), held_as=jnp.bfloat16):
    values = jax.random.normal(stream_key, extent, jnp.float32) * spread
    if len(cuts) > 0:
        values = block_scale(stream_key, extent, cuts, -0.22, 0.18) * values
    return jnp.clip(values, min=-limit, max=limit).astype(held_as)


def setup_inputs(seed: int = 0) -> dict:
    streams_of = jax.random.split(jax.random.key(seed), 6)
    return {
        "clip_frames": centred(streams_of[0], (GROUPS, FRAMES, H, WW, C), 1.0, 6.0, ((0, 4), (2, 8))),
        "segments": jax.vmap(lambda own: jnp.searchsorted(jnp.cumsum(ragged(own, FRAMES // 4 + 1, FRAMES, FRAMES // 2, 1)), jnp.arange(FRAMES), side="right"))(jax.random.split(streams_of[1], GROUPS)).reshape((GROUPS, FRAMES)).astype(jnp.int32),
        "weight_first": centred(streams_of[2], (27 * C, C), (27 * C) ** -0.5, 0.109375),
        "weight_second": centred(streams_of[3], (27 * C, C), (27 * C) ** -0.5, 0.109375),
        "cotangent": centred(streams_of[4], (GROUPS, FRAMES, H // 2, WW // 2, C), 1.0, 6.0, ((0, 4), (2, 8))),
    }


def make_masks(clip_ids):
    frame_count = clip_ids.shape[0]
    result = []
    for delay_step in range(3):
        earlier = jnp.concatenate([jnp.full((delay_step,), -1, jnp.int32), clip_ids[:frame_count - delay_step].astype(jnp.int32)])
        result.append(earlier == clip_ids.astype(jnp.int32))
    return result

def move_frames(field, delay_step, reverse):
    if delay_step == 0:
        return field
    filler = jnp.zeros((delay_step,) + field.shape[1:], field.dtype)
    if reverse:
        return jnp.concatenate([field[delay_step:], filler], axis=0)
    return jnp.concatenate([filler, field[:field.shape[0] - delay_step]], axis=0)

def tap_columns(padded, frame_masks, reverse, row_count, col_count):
    channels = padded.shape[-1]
    pieces = []
    for delay_step in range(3):
        keep = frame_masks[delay_step]
        if reverse:
            keep = move_frames(keep, delay_step, True)
        moved = jnp.where(keep[:, None, None, None], move_frames(padded, delay_step, reverse), jnp.zeros((), padded.dtype))
        for row_tap in range(3):
            for col_tap in range(3):
                row_at = 2 - row_tap if reverse else row_tap
                col_at = 2 - col_tap if reverse else col_tap
                pieces.append(moved[:, row_at:row_at + row_count, col_at:col_at + col_count, :])
    return jnp.concatenate(pieces, axis=-1).reshape(-1, 27 * channels)

def flip_kernel(kernel):
    channels = kernel.shape[1]
    return kernel.reshape(27, channels, channels).transpose(0, 2, 1).reshape(27 * channels, channels)

def pad_both(field):
    return jnp.pad(field, ((0, 0), (1, 1), (1, 1), (0, 0)))

def one_group(frames_one, clip_ids, cot_one, weight_first, weight_second):
    frame_count, row_count, col_count, channels = frames_one.shape
    shape_four = (frame_count, row_count, col_count, channels)
    frame_masks = make_masks(clip_ids)
    columns_in = tap_columns(pad_both(frames_one), frame_masks, False, row_count, col_count)
    first_out = jnp.dot(columns_in, weight_first, preferred_element_type=jnp.float32)
    hidden = jax.nn.silu(first_out).astype(jnp.bfloat16).reshape(shape_four)
    columns_hidden = tap_columns(pad_both(hidden), frame_masks, False, row_count, col_count)
    second_out = jnp.dot(columns_hidden, weight_second, preferred_element_type=jnp.float32)
    summed = frames_one.astype(jnp.float32) + second_out.reshape(shape_four)
    pooled = summed.reshape(frame_count, row_count // 2, 2, col_count // 2, 2, channels).mean(axis=(2, 4))
    grad_out = jnp.repeat(jnp.repeat(cot_one, 2, axis=1), 2, axis=2) * jnp.bfloat16(0.25)
    columns_grad = tap_columns(pad_both(grad_out), frame_masks, True, row_count, col_count)
    grad_hidden = jnp.dot(columns_grad, flip_kernel(weight_second), preferred_element_type=jnp.float32)
    sigma = jax.nn.sigmoid(first_out)
    grad_act = (grad_hidden * sigma * (1.0 + first_out * (1.0 - sigma))).astype(jnp.bfloat16)
    columns_back = tap_columns(pad_both(grad_act.reshape(shape_four)), frame_masks, True, row_count, col_count)
    back_term = jnp.dot(columns_back, flip_kernel(weight_first), preferred_element_type=jnp.float32)
    input_grad = grad_out.astype(jnp.float32) + back_term.reshape(shape_four)
    grad_second = jnp.dot(columns_hidden.T, grad_out.reshape(-1, channels), preferred_element_type=jnp.float32)
    grad_first = jnp.dot(columns_in.T, grad_act, preferred_element_type=jnp.float32)
    return (pooled, input_grad, grad_first, grad_second)

def reference(clip_frames, segments, weight_first, weight_second, cotangent):

    def step_group(operands):
        return one_group(operands[0], operands[1], operands[2], weight_first, weight_second)
    pooled, input_grad, firsts, seconds = lax.map(step_group, (clip_frames, segments, cotangent))
    scale = 1.0 / math.sqrt(GROUPS * FRAMES * H * WW)
    grad_first = lax.optimization_barrier(jnp.sum(firsts, axis=0)) * scale
    grad_second = lax.optimization_barrier(jnp.sum(seconds, axis=0)) * scale
    return (pooled, input_grad, grad_first, grad_second)
```

```python
import functools
import math

import jax
import jax.numpy as jnp
from jax import lax
from jax.experimental import pallas as pl
from jax.experimental.pallas import tpu as pltpu
from jax.sharding import PartitionSpec as P

MESH = pl.DeviceIdType.MESH
F32 = jnp.float32
BF16 = jnp.bfloat16


def up16(n):
    return -(-n // 16) * 16


def shifted_cols(cells, step):
    if step == 0:
        return cells
    cols = cells.shape[2]
    col = lax.broadcasted_iota(jnp.int32, cells.shape, 2)
    moved = pltpu.roll(cells, (-step) % cols, 2)
    keep = (col < cols - 1) if step == 1 else (col > 0)
    return jnp.where(keep, moved, 0.0)


def fill_columns(dst, cells, same, reverse):
    rows, frames, cols, ch = cells.shape
    for ci in range(3):
        moved = shifted_cols(cells, (1 - ci) if reverse else (ci - 1))
        for t in range(3):
            zero = jnp.zeros((rows, cols, ch), F32)
            parts = []
            for f in range(frames):
                src = f + t if reverse else f - t
                if src < 0 or src >= frames:
                    parts.append(zero)
                elif t == 0:
                    parts.append(moved[:, src])
                else:
                    parts.append(moved[:, src] * same[t][max(f, src)])
            block = jnp.stack(parts, axis=1).reshape(rows * frames * cols, ch)
            at = (t * 3 + ci) * ch
            dst[:, at : at + ch] = block.astype(BF16)


def conv_dots(cols_ref, w_ref, start, rows, slab, reverse):
    acc = None
    span = w_ref.shape[1] * 3
    for t in range(3):
        for a in range(3):
            at = (start + (2 - a if reverse else a)) * slab
            term = jnp.dot(
                cols_ref[at : at + rows * slab, t * span : (t + 1) * span],
                w_ref[(t * 3 + a) * span : (t * 3 + a + 1) * span, :],
                preferred_element_type=F32,
            )
            acc = term if acc is None else acc + term
    return acc


def kernel(
    cfg,
    seg, x_hbm, w1_hbm, w2_hbm, c_hbm,
    pooled_hbm, in_grad_hbm, out1, out2,
    pooled, in_grad, out_sem, x_in, w1, w2, c_in, g_tmp, in_sem, x_halo, g_halo, cols_x, cols_h, cols_g, cols_a, w1t, w2t, pool_tmp,
    flat1, flat2, send_a, recv_a, sum_a, send_b, recv_b, sum_b, send_c, recv_c, fin,
    h_send, h_recv, a_send, a_recv, b_send, b_recv, c_send, c_recv, d_send, d_recv,
):
    n_tile, n_dp, share, chunk, scale = cfg
    n_z = n_tile // 2
    rows, frames, cols, ch = x_in.shape
    slab = frames * cols
    tile = lax.axis_index("tile")
    dp = lax.axis_index("dp")
    core = lax.rem(tile, 2)
    z = lax.div(tile, 2)
    flats = (flat1, flat2)
    outs = (out1, out2)

    load_x = [
        pltpu.make_async_copy(x_hbm.at[0, :, r], x_in.at[r], in_sem.at[2 + r]) for r in range(rows)
    ]
    load_c = [
        pltpu.make_async_copy(c_hbm.at[0, :, r], c_in.at[r], in_sem.at[2 + rows + r])
        for r in range(rows // 2)
    ]
    load_w1 = pltpu.make_async_copy(w1_hbm, w1, in_sem.at[0])
    load_w2 = pltpu.make_async_copy(w2_hbm, w2, in_sem.at[1])
    for copy in load_x + load_c:
        copy.start()
    load_w1.start()
    load_w2.start()

    barrier = pltpu.get_barrier_semaphore()

    def greet(peer):
        pl.semaphore_signal(barrier, inc=1, device_id=peer, device_id_type=MESH)

    @pl.when(tile > 0)
    def _():
        greet({"tile": tile - 1})

    @pl.when(tile < n_tile - 1)
    def _():
        greet({"tile": tile + 1})

    for i in range(1, n_dp):
        greet({"dp": lax.rem(dp + i, n_dp)})
    for j in range(1, n_z):
        greet({"tile": 2 * lax.rem(z + j, n_z) + core})

    span = 3 * ch

    def flip(src, dst):
        for tap in range(27):
            dst[tap * ch : (tap + 1) * ch, :] = src[tap * ch : (tap + 1) * ch, :].T

    for g in range(2):
        if sum_a.shape[2] > share:
            sum_a[g, :, share:, :] = jnp.zeros((n_z, sum_a.shape[2] - share, ch), F32)
        if send_a.shape[2] > share:
            send_a[g, :, share:, :] = jnp.zeros((n_z, send_a.shape[2] - share, ch), BF16)

    @pl.when(tile == 0)
    def _():
        x_halo[0] = jnp.zeros(x_halo.shape[1:], BF16)
        g_halo[0] = jnp.zeros(g_halo.shape[1:], BF16)

    @pl.when(tile == n_tile - 1)
    def _():
        x_halo[1] = jnp.zeros(x_halo.shape[1:], BF16)
        g_halo[1] = jnp.zeros(g_halo.shape[1:], BF16)

    for copy in load_x + load_c:
        copy.wait()
    beside = jnp.where(tile > 0, 1, 0) + jnp.where(tile < n_tile - 1, 1, 0)
    pl.semaphore_wait(barrier, n_dp - 1 + n_z - 1 + beside)

    g_rows = c_in.shape[0]

    def halo(side):
        peer = {"tile": tile - 1 if side == 0 else tile + 1}
        return (
            pltpu.make_async_remote_copy(
                src_ref=x_in.at[0:2] if side == 0 else x_in.at[rows - 2 : rows],
                dst_ref=x_halo.at[1 - side],
                send_sem=h_send.at[side], recv_sem=h_recv.at[1 - side],
                device_id=peer, device_id_type=MESH,
            ),
            pltpu.make_async_remote_copy(
                src_ref=c_in.at[0:1] if side == 0 else c_in.at[g_rows - 1 : g_rows],
                dst_ref=g_halo.at[1 - side],
                send_sem=h_send.at[2 + side], recv_sem=h_recv.at[2 + 1 - side],
                device_id=peer, device_id_type=MESH,
            ),
        )

    @pl.when(tile > 0)
    def _():
        for copy in halo(0):
            copy.start()

    @pl.when(tile < n_tile - 1)
    def _():
        for copy in halo(1):
            copy.start()

    load_w1.wait()
    load_w2.wait()
    flip(w2, w2t)
    flip(w1, w1t)
    same = [None]
    for t in range(1, 3):
        same.append(
            [None] * t
            + [jnp.where(seg[0, f] == seg[0, f - t], 1.0, 0.0).astype(F32) for f in range(t, frames)]
        )

    @pl.when(tile > 0)
    def _():
        for copy in halo(0):
            copy.wait_send()
        for copy in halo(1):
            copy.wait_recv()

    @pl.when(tile < n_tile - 1)
    def _():
        for copy in halo(1):
            copy.wait_send()
        for copy in halo(0):
            copy.wait_recv()

    def four(v):
        return v.reshape(v.shape[0], frames, cols, ch)

    mine = x_in[...].astype(F32)
    x_all = jnp.concatenate([x_halo[0].astype(F32), mine, x_halo[1].astype(F32)], axis=0)
    fill_columns(cols_x, x_all, same, False)
    c_all = jnp.concatenate([g_halo[0], c_in[...], g_halo[1]], axis=0).astype(F32) * 0.25
    half = (g_rows + 2) * slab // 2
    c_all = c_all.reshape(half, ch)
    g_tmp[pl.ds(0, half, stride=2), :] = c_all
    g_tmp[pl.ds(1, half, stride=2), :] = c_all
    g_all = g_tmp[...].reshape(g_rows + 2, slab, ch)
    g_all = jnp.stack([g_all, g_all], axis=1).reshape(2 * g_all.shape[0], slab, ch)

    wide = rows + 2
    first = conv_dots(cols_x, w1, 0, wide, slab, False)
    sigma = 1.0 / (1.0 + jnp.exp(-first))
    top = jnp.where(tile > 0, 1.0, 0.0).astype(F32)
    low = jnp.where(tile < n_tile - 1, 1.0, 0.0).astype(F32)

    def edges(v):
        v = v.reshape(wide, slab, ch)
        return jnp.concatenate([v[:1] * top, v[1:-1], v[-1:] * low], axis=0)

    def kernel_grad(flat, cols_ref, start, g):
        for t in range(3):
            for a in range(3):
                at = (start + a) * slab
                flat[(t * 3 + a) * span : (t * 3 + a + 1) * span, :] = lax.dot_general(
                    cols_ref[at : at + rows * slab, t * span : (t + 1) * span],
                    g,
                    (((0,), (0,)), ((), ())),
                    preferred_element_type=F32,
                )

    def copies_a(g):
        return [
            pltpu.make_async_remote_copy(
                src_ref=send_a.at[g, k],
                dst_ref=recv_a.at[g, k],
                send_sem=a_send.at[g, k], recv_sem=a_recv.at[g, k],
                device_id={"tile": tile + 1 - 2 * core}, device_id_type=MESH,
            )
            for k in range(n_z)
        ]

    def copies_b(g):
        return [
            pltpu.make_async_remote_copy(
                src_ref=send_b.at[g, i - 1], dst_ref=recv_b.at[g, i - 1],
                send_sem=b_send.at[g, i - 1], recv_sem=b_recv.at[g, i - 1],
                device_id={"dp": lax.rem(dp + i, n_dp)}, device_id_type=MESH,
            )
            for i in range(1, n_dp)
        ]

    def copies_c(g):
        return [
            pltpu.make_async_remote_copy(
                src_ref=send_c.at[g, j - 1], dst_ref=recv_c.at[g, j - 1],
                send_sem=c_send.at[g, j - 1], recv_sem=c_recv.at[g, j - 1],
                device_id={"tile": 2 * lax.rem(z + j, n_z) + core}, device_id_type=MESH,
            )
            for j in range(1, n_z)
        ]

    def part(q):
        return pl.ds(pl.multiple_of(q * chunk, 16), chunk)

    def copies_d(g):
        return [
            pltpu.make_async_remote_copy(
                src_ref=fin.at[g, part(dp)], dst_ref=fin.at[g, part(dp)],
                send_sem=d_send.at[g, i - 1], recv_sem=d_recv.at[g, i - 1],
                device_id={"dp": lax.rem(dp + i, n_dp)}, device_id_type=MESH,
            )
            for i in range(1, n_dp)
        ]

    def start(copies):
        for copy in copies:
            copy.start()

    def wait(copies):
        for copy in copies:
            copy.wait()

    def step_b(g):
        wait(copies_a(g))
        for k in range(n_z):
            own = flats[g][pl.ds(pl.multiple_of((2 * k + core) * share, 8), share), :]
            sum_a[g, k, 0:share, :] = own + recv_a[g, k, 0:share].astype(F32)
        for i in range(1, n_dp):
            send_b[g, i - 1] = sum_a[g, :, part(lax.rem(dp + i, n_dp)), :].astype(BF16)
        start(copies_b(g))

    def step_c(g):
        wait(copies_b(g))
        total = sum_a[g, :, part(dp), :]
        for i in range(1, n_dp):
            total = total + recv_b[g, i - 1].astype(F32)
        sum_b[g] = total
        for j in range(1, n_z):
            send_c[g, j - 1] = sum_b[g, lax.rem(z + j, n_z)].astype(BF16)
        start(copies_c(g))

    def step_d(g):
        wait(copies_c(g))
        total = sum_b[g, z]
        for j in range(1, n_z):
            total = total + recv_c[g, j - 1].astype(F32)
        fin[g, part(dp), :] = total * scale
        start(copies_d(g))

    def step_a(g):
        for k, copy in enumerate(copies_a(g)):
            at = pl.ds(pl.multiple_of((2 * k + 1 - core) * share, 8), share)
            send_a[g, k, 0:share, :] = flats[g][at, :].astype(BF16)
            copy.start()

    hidden = edges(first * sigma)
    fill_columns(cols_h, four(hidden), same, False)
    g_own = g_all[2 : 2 + rows].reshape(rows * slab, ch)
    kernel_grad(flat2, cols_h, 0, g_own.astype(BF16))
    step_a(1)
    fill_columns(cols_g, four(g_all), same, True)
    hidden_grad = conv_dots(cols_g, w2t, 0, wide, slab, True)
    act = edges(hidden_grad * sigma * (1.0 + first * (1.0 - sigma)))
    act_own = act[1 : 1 + rows].reshape(rows * slab, ch).astype(BF16)

    step_b(1)
    kernel_grad(flat1, cols_x, 1, act_own)
    step_a(0)
    fill_columns(cols_a, four(act), same, True)
    step_b(0)
    second = conv_dots(cols_h, w2, 0, rows, slab, False)
    summed = mine.reshape(rows, slab, ch) + second.reshape(rows, slab, ch)
    pairs = rows // 2
    for i in range(pairs):
        pool_tmp[i * slab : (i + 1) * slab, :] = summed[2 * i] + summed[2 * i + 1]
    for i in range(pairs):
        for f in range(frames):
            at = i * slab + f * cols
            pooled[f, i] = 0.25 * (
                pool_tmp[pl.ds(at, cols // 2, stride=2), :]
                + pool_tmp[pl.ds(at + 1, cols // 2, stride=2), :]
            )
    put_pooled = pltpu.make_async_copy(pooled, pooled_hbm.at[0], out_sem.at[2])
    put_pooled.start()
    step_c(1)
    back = conv_dots(cols_a, w1t, 0, rows, slab, True)
    total = (g_own + back).reshape(rows, frames, cols, ch)
    for r in range(rows):
        in_grad[:, r] = total[r]
    put_grad = pltpu.make_async_copy(in_grad, in_grad_hbm.at[0], out_sem.at[3])
    put_grad.start()
    step_c(0)
    step_d(1)
    step_d(0)
    puts = [pltpu.make_async_copy(fin.at[g, 0:share], outs[g], out_sem.at[g]) for g in range(2)]
    for g in (1, 0):
        wait(copies_d(g))
        puts[g].start()
    put_pooled.wait()
    put_grad.wait()
    for g in (1, 0):
        puts[g].wait()


def hand_out(*refs):
    held, load_sem, store_sem = refs[8:12], refs[12], refs[13]
    loads = [pltpu.make_async_copy(refs[i], held[i], load_sem.at[i]) for i in range(4)]
    stores = [pltpu.make_async_copy(held[i], refs[4 + i], store_sem.at[i]) for i in range(4)]
    for copy in loads:
        copy.start()
    for i in (0, 2, 3, 1):
        loads[i].wait()
        stores[i].start()
    for copy in stores:
        copy.wait()


def local(n_tile, n_dp, clip_frames, segments, weight_first, weight_second, cotangent):
    _, frames, rows, cols, ch = clip_frames.shape
    slab = frames * cols
    taps = weight_first.shape[0]
    share = taps // n_tile
    chunk = up16(-(-share // n_dp))
    n_z = n_tile // 2
    scale = 1.0 / math.sqrt(n_dp * n_tile * rows * slab)
    vmem = pl.BlockSpec(memory_space=pltpu.VMEM)
    cells = rows * slab
    sem = pltpu.SemaphoreType.DMA
    anywhere = pl.BlockSpec(memory_space=pltpu.HBM)
    shapes = (
        jax.ShapeDtypeStruct((1, frames, rows // 2, cols // 2, ch), F32),
        jax.ShapeDtypeStruct((1, frames, rows, cols, ch), F32),
        jax.ShapeDtypeStruct((share, ch), F32),
        jax.ShapeDtypeStruct((share, ch), F32),
    )
    results = pl.pallas_call(
        functools.partial(kernel, (n_tile, n_dp, share, chunk, scale)),
        out_shape=shapes,
        in_specs=[pl.BlockSpec(memory_space=pltpu.SMEM)] + [anywhere] * 4,
        out_specs=(anywhere,) * 4,
        scratch_shapes=[
            pltpu.VMEM((frames, rows // 2, cols // 2, ch), F32),
            pltpu.VMEM((frames, rows, cols, ch), F32),
            sem((4,)),
            pltpu.VMEM((rows, frames, cols, ch), BF16),
            pltpu.VMEM((taps, ch), BF16),
            pltpu.VMEM((taps, ch), BF16),
            pltpu.VMEM((rows // 2, frames, cols // 2, ch), BF16),
            pltpu.VMEM(((rows // 2 + 2) * slab, ch), F32),
            sem((2 + rows + rows // 2,)),
            pltpu.VMEM((2, 2, frames, cols, ch), BF16),
            pltpu.VMEM((2, 1, frames, cols // 2, ch), BF16),
            pltpu.VMEM(((rows + 4) * slab, 9 * ch), BF16),
            pltpu.VMEM(((rows + 2) * slab, 9 * ch), BF16),
            pltpu.VMEM(((rows + 4) * slab, 9 * ch), BF16),
            pltpu.VMEM(((rows + 2) * slab, 9 * ch), BF16),
            pltpu.VMEM((taps, ch), BF16),
            pltpu.VMEM((taps, ch), BF16),
            pltpu.VMEM((cells // 2, ch), F32),
            pltpu.VMEM((taps, ch), F32),
            pltpu.VMEM((taps, ch), F32),
            pltpu.VMEM((2, n_z, up16(share), ch), BF16),
            pltpu.VMEM((2, n_z, up16(share), ch), BF16),
            pltpu.VMEM((2, n_z, n_dp * chunk, ch), F32),
            pltpu.VMEM((2, n_dp - 1, n_z, chunk, ch), BF16),
            pltpu.VMEM((2, n_dp - 1, n_z, chunk, ch), BF16),
            pltpu.VMEM((2, n_z, chunk, ch), F32),
            pltpu.VMEM((2, n_z - 1, chunk, ch), BF16),
            pltpu.VMEM((2, n_z - 1, chunk, ch), BF16),
            pltpu.VMEM((2, n_dp * chunk, ch), F32),
            sem((4,)), sem((4,)),
            sem((2, n_z)), sem((2, n_z)),
            sem((2, n_dp - 1)), sem((2, n_dp - 1)),
            sem((2, n_z - 1)), sem((2, n_z - 1)),
            sem((2, n_dp - 1)), sem((2, n_dp - 1)),
        ],
        compiler_params=pltpu.CompilerParams(
            collective_id=0, has_side_effects=True, vmem_limit_bytes=60 * 1024 * 1024
        ),
    )(segments, clip_frames, weight_first, weight_second, cotangent)
    return tuple(
        pl.pallas_call(
            hand_out,
            out_shape=shapes,
            in_specs=[pl.BlockSpec(memory_space=pl.ANY)] * 4,
            out_specs=(pl.BlockSpec(memory_space=pl.ANY),) * 4,
            scratch_shapes=[pltpu.VMEM(v.shape, v.dtype) for v in shapes] + [sem((4,))] * 2,
        )(*results)
    )


def solution(mesh):
    return jax.shard_map(
        functools.partial(local, mesh.shape["tile"], mesh.shape["dp"]),
        mesh=mesh,
        in_specs=(
            P("dp", None, "tile", None, None),
            P("dp", None),
            P(),
            P(),
            P("dp", None, "tile", None, None),
        ),
        out_specs=(
            P("dp", None, "tile", None, None),
            P("dp", None, "tile", None, None),
            P("tile", None),
            P("tile", None),
        ),
        check_vma=False,
    )
```

```python
import functools
import math

import jax
import jax.numpy as jnp
from jax import lax
from jax.experimental import pallas as pl
from jax.experimental.pallas import tpu as pltpu
from jax.sharding import PartitionSpec as P

MESH = pl.DeviceIdType.MESH
F32 = jnp.float32
BF16 = jnp.bfloat16


def up16(n):
    return -(-n // 16) * 16


def shifted_cols(cells, step):
    if step == 0:
        return cells
    cols = cells.shape[2]
    col = lax.broadcasted_iota(jnp.int32, cells.shape, 2)
    moved = pltpu.roll(cells, (-step) % cols, 2)
    keep = (col < cols - 1) if step == 1 else (col > 0)
    return jnp.where(keep, moved, 0.0)


def fill_columns(dst, cells, same, reverse):
    rows, frames, cols, ch = cells.shape
    for ci in range(3):
        moved = shifted_cols(cells, (1 - ci) if reverse else (ci - 1))
        for t in range(3):
            zero = jnp.zeros((rows, cols, ch), F32)
            parts = []
            for f in range(frames):
                src = f + t if reverse else f - t
                if src < 0 or src >= frames:
                    parts.append(zero)
                elif t == 0:
                    parts.append(moved[:, src])
                else:
                    parts.append(moved[:, src] * same[t][max(f, src)])
            block = jnp.stack(parts, axis=1).reshape(rows * frames * cols, ch)
            at = (t * 3 + ci) * ch
            dst[:, at : at + ch] = block.astype(BF16)


def conv_dots(cols_ref, w_ref, start, rows, slab, reverse):
    acc = None
    span = w_ref.shape[1] * 3
    for t in range(3):
        for a in range(3):
            at = (start + (2 - a if reverse else a)) * slab
            term = jnp.dot(
                cols_ref[at : at + rows * slab, t * span : (t + 1) * span],
                w_ref[(t * 3 + a) * span : (t * 3 + a + 1) * span, :],
                preferred_element_type=F32,
            )
            acc = term if acc is None else acc + term
    return acc


def kernel(
    cfg,
    seg, x_hbm, w1_hbm, w2_hbm, c_hbm,
    pooled_hbm, in_grad_hbm, out1, out2,
    pooled, in_grad, out_sem, x_in, w1, w2, c_in, g_tmp, in_sem, x_halo, g_halo, cols_x, cols_h, cols_g, cols_a, w1t, w2t, pool_tmp,
    seg_rows, mask_rows, x_out, x_got, hid_out, hid_got, cot_got, act_got, g_got, turned, flat,
    recv_a, sum_a, send_c, recv_c, every, spread, out_v,
    h_send, h_recv, x_send, x_recv, s_send, s_recv, k_send, k_recv, g_send, g_recv, t_send, t_recv,
    a_send, a_recv, c_send, c_recv, d_send, d_recv,
):
    n_tile, n_dp, share, quarter, part, n_tap, scale = cfg
    n_z = n_tile // 2
    rows, frames, cols, ch = x_in.shape
    slab = frames * cols
    tile = lax.axis_index("tile")
    dp = lax.axis_index("dp")
    core = lax.rem(tile, 2)
    z = lax.div(tile, 2)
    taps = w1.shape[0] // ch
    outs = (out1, out2)
    wide = rows + 2
    cells = rows * slab
    lanes = wide * slab
    block = n_tap * part

    load_x = [
        pltpu.make_async_copy(x_hbm.at[0, :, r], x_in.at[r], in_sem.at[2 + r]) for r in range(rows)
    ]
    load_c = [
        pltpu.make_async_copy(c_hbm.at[0, :, r], c_in.at[r], in_sem.at[2 + rows + r])
        for r in range(rows // 2)
    ]
    load_w1 = pltpu.make_async_copy(w1_hbm, w1, in_sem.at[0])
    load_w2 = pltpu.make_async_copy(w2_hbm, w2, in_sem.at[1])
    for copy in load_x + load_c:
        copy.start()
    load_w1.start()
    load_w2.start()

    barrier = pltpu.get_barrier_semaphore()

    def greet(peer):
        pl.semaphore_signal(barrier, inc=1, device_id=peer, device_id_type=MESH)

    @pl.when(tile > 0)
    def _():
        greet({"tile": tile - 1})

    @pl.when(tile < n_tile - 1)
    def _():
        greet({"tile": tile + 1})

    for i in range(1, n_dp):
        greet({"dp": lax.rem(dp + i, n_dp)})
    for j in range(1, n_z):
        greet({"tile": 2 * lax.rem(z + j, n_z) + core})

    span = 3 * ch

    def flip(src, dst):
        for tap in range(27):
            dst[tap * ch : (tap + 1) * ch, :] = src[tap * ch : (tap + 1) * ch, :].T

    if part > quarter:
        x_out[:, quarter:, :] = jnp.zeros((n_dp, part - quarter, lanes), BF16)
        hid_out[:, quarter:, :] = jnp.zeros((n_dp, part - quarter, lanes), BF16)
    lane = lax.broadcasted_iota(jnp.int32, (16, lanes), 1)
    frame = lax.rem(lax.div(lane, cols), frames)
    number = jnp.zeros((16, lanes), F32)
    for f in range(frames):
        number = jnp.where(frame == f, seg[0, f].astype(F32), number)
    seg_rows[dp] = number.astype(BF16)

    @pl.when(tile == 0)
    def _():
        x_halo[0] = jnp.zeros(x_halo.shape[1:], BF16)
        g_halo[0] = jnp.zeros(g_halo.shape[1:], BF16)

    @pl.when(tile == n_tile - 1)
    def _():
        x_halo[1] = jnp.zeros(x_halo.shape[1:], BF16)
        g_halo[1] = jnp.zeros(g_halo.shape[1:], BF16)

    for copy in load_x + load_c:
        copy.wait()
    beside = jnp.where(tile > 0, 1, 0) + jnp.where(tile < n_tile - 1, 1, 0)
    pl.semaphore_wait(barrier, n_dp - 1 + n_z - 1 + beside)

    g_rows = c_in.shape[0]

    def halo(side):
        peer = {"tile": tile - 1 if side == 0 else tile + 1}
        return (
            pltpu.make_async_remote_copy(
                src_ref=x_in.at[0:2] if side == 0 else x_in.at[rows - 2 : rows],
                dst_ref=x_halo.at[1 - side],
                send_sem=h_send.at[side], recv_sem=h_recv.at[1 - side],
                device_id=peer, device_id_type=MESH,
            ),
            pltpu.make_async_remote_copy(
                src_ref=c_in.at[0:1] if side == 0 else c_in.at[g_rows - 1 : g_rows],
                dst_ref=g_halo.at[1 - side],
                send_sem=h_send.at[2 + side], recv_sem=h_recv.at[2 + 1 - side],
                device_id=peer, device_id_type=MESH,
            ),
        )

    @pl.when(tile > 0)
    def _():
        for copy in halo(0):
            copy.start()

    @pl.when(tile < n_tile - 1)
    def _():
        for copy in halo(1):
            copy.start()

    def to_dp(src, dst, sends, recvs):
        return [
            pltpu.make_async_remote_copy(
                src_ref=src(lax.rem(dp + i, n_dp)), dst_ref=dst,
                send_sem=sends.at[i - 1], recv_sem=recvs.at[i - 1],
                device_id={"dp": lax.rem(dp + i, n_dp)}, device_id_type=MESH,
            )
            for i in range(1, n_dp)
        ]

    def start(copies):
        for copy in copies:
            copy.start()

    def wait(copies):
        for copy in copies:
            copy.wait()

    copies_cot = to_dp(lambda q: c_in, cot_got.at[dp], k_send, k_recv)
    copies_seg = to_dp(lambda q: seg_rows.at[dp], seg_rows.at[dp], s_send, s_recv)
    start(copies_cot)
    start(copies_seg)
    cot_got[dp] = c_in[...]

    load_w1.wait()
    load_w2.wait()
    flip(w2, w2t)
    flip(w1, w1t)
    same = [None]
    for t in range(1, 3):
        same.append(
            [None] * t
            + [jnp.where(seg[0, f] == seg[0, f - t], 1.0, 0.0).astype(F32) for f in range(t, frames)]
        )

    @pl.when(tile > 0)
    def _():
        for copy in halo(0):
            copy.wait_send()
        for copy in halo(1):
            copy.wait_recv()

    @pl.when(tile < n_tile - 1)
    def _():
        for copy in halo(1):
            copy.wait_send()
        for copy in halo(0):
            copy.wait_recv()

    def four(v):
        return v.reshape(v.shape[0], frames, cols, ch)

    mine = x_in[...].astype(F32)
    x_all = jnp.concatenate([x_halo[0].astype(F32), mine, x_halo[1].astype(F32)], axis=0)
    copies_x = to_dp(lambda q: x_out.at[q], x_got.at[dp], x_send, x_recv)
    copies_hid = to_dp(lambda q: hid_out.at[q], hid_got.at[dp], t_send, t_recv)
    copies_act = to_dp(lambda q: act_got.at[dp], act_got.at[dp], g_send, g_recv)

    def deal(v, out, got, copies):
        v = v.reshape(lanes, ch).T.astype(BF16)
        for q in range(n_dp):
            out[q, 0:quarter, :] = v[q * quarter : (q + 1) * quarter]
        start(copies)
        got[dp] = out[dp]

    deal(x_all[1 : 1 + wide], x_out, x_got, copies_x)
    fill_columns(cols_x, x_all, same, False)
    c_all = jnp.concatenate([g_halo[0], c_in[...], g_halo[1]], axis=0).astype(F32) * 0.25
    half = (g_rows + 2) * slab // 2
    c_all = c_all.reshape(half, ch)
    g_tmp[pl.ds(0, half, stride=2), :] = c_all
    g_tmp[pl.ds(1, half, stride=2), :] = c_all
    g_all = g_tmp[...].reshape(g_rows + 2, slab, ch)
    g_all = jnp.stack([g_all, g_all], axis=1).reshape(2 * g_all.shape[0], slab, ch)

    first = conv_dots(cols_x, w1, 0, wide, slab, False)
    sigma = 1.0 / (1.0 + jnp.exp(-first))
    top = jnp.where(tile > 0, 1.0, 0.0).astype(F32)
    low = jnp.where(tile < n_tile - 1, 1.0, 0.0).astype(F32)

    def edges(v):
        v = v.reshape(wide, slab, ch)
        return jnp.concatenate([v[:1] * top, v[1:-1], v[-1:] * low], axis=0)

    def tap_0(to):
        return jnp.minimum(lax.div(share * to, ch), taps - n_tap)

    def window(to):
        return pl.ds(pl.multiple_of(tap_0(to) * part, 16), block)

    def copies_a(g):
        return [
            pltpu.make_async_remote_copy(
                src_ref=flat.at[g, window(2 * k + 1 - core)], dst_ref=recv_a.at[g, k],
                send_sem=a_send.at[g, k], recv_sem=a_recv.at[g, k],
                device_id={"tile": tile + 1 - 2 * core}, device_id_type=MESH,
            )
            for k in range(n_z)
        ]

    def copies_c(g):
        return [
            pltpu.make_async_remote_copy(
                src_ref=send_c.at[g, j - 1], dst_ref=recv_c.at[g, j - 1],
                send_sem=c_send.at[g, j - 1], recv_sem=c_recv.at[g, j - 1],
                device_id={"tile": 2 * lax.rem(z + j, n_z) + core}, device_id_type=MESH,
            )
            for j in range(1, n_z)
        ]

    def copies_d(g):
        return to_dp(lambda q: every.at[g, dp], every.at[g, dp], d_send.at[g], d_recv.at[g])

    def sender(i):
        return lax.rem(dp + n_dp - i, n_dp)

    def make_masks(d):
        number = seg_rows[d].astype(F32)[0:8]
        at = lax.broadcasted_iota(jnp.int32, (8, lanes), 1)
        when = lax.rem(lax.div(at, cols), frames)
        col = lax.rem(at, cols)
        for t in range(3):
            keep = jnp.ones((8, lanes), F32)
            if t > 0:
                keep = jnp.where(number == pltpu.roll(number, t * cols, 1), 1.0, 0.0)
                keep = jnp.where(when >= t, keep, 0.0)
            for b in range(3):
                inside = jnp.where((col + (b - 1) >= 0) & (col + (b - 1) < cols), keep, 0.0)
                mask_rows[d, t * 3 + b] = inside

    def turn(g, d, got):
        v = got[d].astype(F32)[0:part]
        for t in range(3):
            for b in range(3):
                shift = t * cols - (b - 1)
                moved = v if shift == 0 else pltpu.roll(v, shift % lanes, 1)
                if t > 0 or b != 1:
                    keep = mask_rows[d, t * 3 + b]
                    moved = moved * jnp.concatenate([keep] * (part // 8), axis=0)
                middle = pltpu.roll(moved, lanes - slab, 1)
                low = moved[:, 0:cells].astype(BF16)
                mid = middle[:, 0:cells].astype(BF16)
                high = moved[:, 2 * slab :].astype(BF16)
                for a, w in enumerate((low, mid, high)):
                    at = ((t * 3 + a) * 3 + b) * part
                    turned[g, d, at : at + part, :] = w

    def partial_sum(g, d, right, fresh):
        term = jnp.dot(turned[g, d], right, preferred_element_type=F32)
        flat[g] = term if fresh else flat[g] + term

    def step_b(g):
        wait(copies_a(g))
        for k in range(n_z):
            sum_a[g, k] = flat[g, window(2 * k + core), :] + recv_a[g, k]
        for j in range(1, n_z):
            send_c[g, j - 1] = sum_a[g, lax.rem(z + j, n_z)].astype(BF16)
        start(copies_c(g))

    def step_c(g):
        wait(copies_c(g))
        total = sum_a[g, z]
        for j in range(1, n_z):
            total = total + recv_c[g, j - 1].astype(F32)
        every[g, dp] = (total * scale).astype(BF16)
        start(copies_d(g))

    def step_d(g):
        wait(copies_d(g))
        for q in range(n_dp):
            v = every[g, q].astype(F32)
            for i in range(n_tap):
                at = i * ch + q * quarter
                spread[g, at : at + quarter, :] = v[i * part : i * part + quarter]
        at = pl.multiple_of(share * tile - ch * tap_0(tile), 8)
        out_v[g] = spread[g, pl.ds(at, share), :]
        copy = pltpu.make_async_copy(out_v.at[g], outs[g], out_sem.at[g])
        copy.start()
        return copy

    hidden = edges(first * sigma)
    deal(hidden, hid_out, hid_got, copies_hid)
    g_own = g_all[2 : 2 + rows].reshape(cells, ch)
    fill_columns(cols_g, four(g_all), same, True)
    hidden_grad = conv_dots(cols_g, w2t, 0, wide, slab, True)
    act = edges(hidden_grad * sigma * (1.0 + first * (1.0 - sigma)))
    act_got[dp] = act[1 : 1 + rows].reshape(cells, ch).astype(BF16)
    start(copies_act)

    wait(copies_seg)
    for d in range(n_dp):
        make_masks(d)
    wait(copies_cot)
    for d in range(n_dp):
        v = (cot_got[d].astype(F32) * 0.25).reshape(cells // 4, ch)
        g_tmp[pl.ds(0, cells // 4, stride=2), :] = v
        g_tmp[pl.ds(1, cells // 4, stride=2), :] = v
        v = g_tmp[0 : cells // 2, :].astype(BF16).reshape(rows // 2, slab, ch)
        g_got[d] = jnp.stack([v, v], axis=1).reshape(cells, ch)
    wait(copies_x)
    for d in range(n_dp):
        turn(0, d, x_got)
    fill_columns(cols_h, four(hidden), same, False)
    for i in range(n_dp):
        if i > 0:
            copies_hid[i - 1].wait()
        turn(1, sender(i), hid_got)
        partial_sum(1, sender(i), g_got[sender(i)], i == 0)
    start(copies_a(1))
    for i in range(n_dp):
        if i > 0:
            copies_act[i - 1].wait()
        partial_sum(0, sender(i), act_got[sender(i)], i == 0)
    start(copies_a(0))
    step_b(1)
    step_b(0)

    second = conv_dots(cols_h, w2, 0, rows, slab, False)
    summed = mine.reshape(rows, slab, ch) + second.reshape(rows, slab, ch)
    pairs = rows // 2
    for i in range(pairs):
        pool_tmp[i * slab : (i + 1) * slab, :] = summed[2 * i] + summed[2 * i + 1]
    for i in range(pairs):
        for f in range(frames):
            at = i * slab + f * cols
            pooled[f, i] = 0.25 * (
                pool_tmp[pl.ds(at, cols // 2, stride=2), :]
                + pool_tmp[pl.ds(at + 1, cols // 2, stride=2), :]
            )
    put_pooled = pltpu.make_async_copy(pooled, pooled_hbm.at[0], out_sem.at[2])
    put_pooled.start()
    fill_columns(cols_a, four(act), same, True)
    back = conv_dots(cols_a, w1t, 0, rows, slab, True)
    total = (g_own + back).reshape(rows, frames, cols, ch)
    for r in range(rows):
        in_grad[:, r] = total[r]
    put_grad = pltpu.make_async_copy(in_grad, in_grad_hbm.at[0], out_sem.at[3])
    put_grad.start()
    step_c(1)
    step_c(0)
    puts = [put_pooled, put_grad, step_d(1), step_d(0)]
    for copy in puts:
        copy.wait()


def hand_out(*refs):
    held, load_sem, store_sem = refs[8:12], refs[12], refs[13]
    loads = [pltpu.make_async_copy(refs[i], held[i], load_sem.at[i]) for i in range(4)]
    stores = [pltpu.make_async_copy(held[i], refs[4 + i], store_sem.at[i]) for i in range(4)]
    for copy in loads:
        copy.start()
    for i in (0, 2, 3, 1):
        loads[i].wait()
        stores[i].start()
    for copy in stores:
        copy.wait()


def local(n_tile, n_dp, clip_frames, segments, weight_first, weight_second, cotangent):
    _, frames, rows, cols, ch = clip_frames.shape
    slab = frames * cols
    taps = weight_first.shape[0]
    share = taps // n_tile
    n_z = n_tile // 2
    quarter = ch // n_dp
    part = up16(quarter)
    n_tap = max(-(-share * (k + 1) // ch) - share * k // ch for k in range(n_tile))
    scale = 1.0 / math.sqrt(n_dp * n_tile * rows * slab)
    vmem = pl.BlockSpec(memory_space=pltpu.VMEM)
    cells = rows * slab
    lanes = (rows + 2) * slab
    sem = pltpu.SemaphoreType.DMA
    anywhere = pl.BlockSpec(memory_space=pltpu.HBM)
    shapes = (
        jax.ShapeDtypeStruct((1, frames, rows // 2, cols // 2, ch), F32),
        jax.ShapeDtypeStruct((1, frames, rows, cols, ch), F32),
        jax.ShapeDtypeStruct((share, ch), F32),
        jax.ShapeDtypeStruct((share, ch), F32),
    )
    results = pl.pallas_call(
        functools.partial(kernel, (n_tile, n_dp, share, quarter, part, n_tap, scale)),
        out_shape=shapes,
        in_specs=[pl.BlockSpec(memory_space=pltpu.SMEM)] + [anywhere] * 4,
        out_specs=(anywhere,) * 4,
        scratch_shapes=[
            pltpu.VMEM((frames, rows // 2, cols // 2, ch), F32),
            pltpu.VMEM((frames, rows, cols, ch), F32),
            sem((4,)),
            pltpu.VMEM((rows, frames, cols, ch), BF16),
            pltpu.VMEM((taps, ch), BF16),
            pltpu.VMEM((taps, ch), BF16),
            pltpu.VMEM((rows // 2, frames, cols // 2, ch), BF16),
            pltpu.VMEM(((rows // 2 + 2) * slab, ch), F32),
            sem((2 + rows + rows // 2,)),
            pltpu.VMEM((2, 2, frames, cols, ch), BF16),
            pltpu.VMEM((2, 1, frames, cols // 2, ch), BF16),
            pltpu.VMEM(((rows + 4) * slab, 9 * ch), BF16),
            pltpu.VMEM(((rows + 2) * slab, 9 * ch), BF16),
            pltpu.VMEM(((rows + 4) * slab, 9 * ch), BF16),
            pltpu.VMEM(((rows + 2) * slab, 9 * ch), BF16),
            pltpu.VMEM((taps, ch), BF16),
            pltpu.VMEM((taps, ch), BF16),
            pltpu.VMEM((cells // 2, ch), F32),
            pltpu.VMEM((n_dp, 16, lanes), BF16),
            pltpu.VMEM((n_dp, 9, 8, lanes), F32),
            pltpu.VMEM((n_dp, part, lanes), BF16),
            pltpu.VMEM((n_dp, part, lanes), BF16),
            pltpu.VMEM((n_dp, part, lanes), BF16),
            pltpu.VMEM((n_dp, part, lanes), BF16),
            pltpu.VMEM((n_dp, rows // 2, frames, cols // 2, ch), BF16),
            pltpu.VMEM((n_dp, cells, ch), BF16),
            pltpu.VMEM((n_dp, cells, ch), BF16),
            pltpu.VMEM((2, n_dp, taps // ch * part, cells), BF16),
            pltpu.VMEM((2, taps // ch * part, ch), F32),
            pltpu.VMEM((2, n_z, n_tap * part, ch), F32),
            pltpu.VMEM((2, n_z, n_tap * part, ch), F32),
            pltpu.VMEM((2, n_z - 1, n_tap * part, ch), BF16),
            pltpu.VMEM((2, n_z - 1, n_tap * part, ch), BF16),
            pltpu.VMEM((2, n_dp, n_tap * part, ch), BF16),
            pltpu.VMEM((2, n_tap * ch, ch), F32),
            pltpu.VMEM((2, share, ch), F32),
            sem((4,)), sem((4,)),
            sem((n_dp - 1,)), sem((n_dp - 1,)),
            sem((n_dp - 1,)), sem((n_dp - 1,)),
            sem((n_dp - 1,)), sem((n_dp - 1,)),
            sem((n_dp - 1,)), sem((n_dp - 1,)),
            sem((n_dp - 1,)), sem((n_dp - 1,)),
            sem((2, n_z)), sem((2, n_z)),
            sem((2, n_z - 1)), sem((2, n_z - 1)),
            sem((2, n_dp - 1)), sem((2, n_dp - 1)),
        ],
        compiler_params=pltpu.CompilerParams(
            collective_id=0, has_side_effects=True, vmem_limit_bytes=60 * 1024 * 1024
        ),
    )(segments, clip_frames, weight_first, weight_second, cotangent)
    return tuple(
        pl.pallas_call(
            hand_out,
            out_shape=shapes,
            in_specs=[pl.BlockSpec(memory_space=pl.ANY)] * 4,
            out_specs=(pl.BlockSpec(memory_space=pl.ANY),) * 4,
            scratch_shapes=[pltpu.VMEM(v.shape, v.dtype) for v in shapes] + [sem((4,))] * 2,
        )(*results)
    )


def solution(mesh):
    return jax.shard_map(
        functools.partial(local, mesh.shape["tile"], mesh.shape["dp"]),
        mesh=mesh,
        in_specs=(
            P("dp", None, "tile", None, None),
            P("dp", None),
            P(),
            P(),
            P("dp", None, "tile", None, None),
        ),
        out_specs=(
            P("dp", None, "tile", None, None),
            P("dp", None, "tile", None, None),
            P("tile", None),
            P("tile", None),
        ),
        check_vma=False,
    )
```

```python
import functools
import math

import jax
import jax.numpy as jnp
from jax import lax
from jax.experimental import pallas as pl
from jax.experimental.pallas import tpu as pltpu
from jax.sharding import PartitionSpec as P

MESH = pl.DeviceIdType.MESH
F32 = jnp.float32
BF16 = jnp.bfloat16


def up16(n):
    return -(-n // 16) * 16


def shifted_cols(cells, step):
    if step == 0:
        return cells
    cols = cells.shape[2]
    col = lax.broadcasted_iota(jnp.int32, cells.shape, 2)
    moved = pltpu.roll(cells, (-step) % cols, 2)
    keep = (col < cols - 1) if step == 1 else (col > 0)
    return jnp.where(keep, moved, 0.0)


def fill_columns(dst, cells, same, reverse):
    rows, frames, cols, ch = cells.shape
    for ci in range(3):
        moved = shifted_cols(cells, (1 - ci) if reverse else (ci - 1))
        for t in range(3):
            zero = jnp.zeros((rows, cols, ch), F32)
            parts = []
            for f in range(frames):
                src = f + t if reverse else f - t
                if src < 0 or src >= frames:
                    parts.append(zero)
                elif t == 0:
                    parts.append(moved[:, src])
                else:
                    parts.append(moved[:, src] * same[t][max(f, src)])
            block = jnp.stack(parts, axis=1).reshape(rows * frames * cols, ch)
            at = (t * 3 + ci) * ch
            dst[:, at : at + ch] = block.astype(BF16)


def conv_dots(cols_ref, w_ref, start, rows, slab, reverse):
    acc = None
    span = w_ref.shape[1] * 3
    for t in range(3):
        for a in range(3):
            at = (start + (2 - a if reverse else a)) * slab
            term = jnp.dot(
                cols_ref[at : at + rows * slab, t * span : (t + 1) * span],
                w_ref[(t * 3 + a) * span : (t * 3 + a + 1) * span, :],
                preferred_element_type=F32,
            )
            acc = term if acc is None else acc + term
    return acc


def kernel(
    cfg,
    seg, x_hbm, w1_hbm, w2_hbm, c_hbm,
    pooled_hbm, in_grad_hbm, out1, out2,
    pooled, in_grad, out_sem, x_in, w1, w2, c_in, g_tmp, in_sem, x_halo, g_halo, cols_x, cols_h, cols_g, cols_a, w1t, w2t, pool_tmp,
    seg_rows, mask_rows, x_out, x_got, hid_out, hid_got, cot_got, act_got, g_got, turned, flat,
    recv_a, sum_a, send_c, recv_c, every, spread, out_v,
    h_send, h_recv, x_send, x_recv, s_send, s_recv, k_send, k_recv, g_send, g_recv, t_send, t_recv,
    a_send, a_recv, c_send, c_recv, d_send, d_recv,
):
    n_tile, n_dp, share, quarter, part, unit, n_unit, scale = cfg
    n_z = n_tile // 2
    rows, frames, cols, ch = x_in.shape
    slab = frames * cols
    tile = lax.axis_index("tile")
    dp = lax.axis_index("dp")
    core = lax.rem(tile, 2)
    z = lax.div(tile, 2)
    taps = w1.shape[0] // ch
    outs = (out1, out2)
    wide = rows + 2
    cells = rows * slab
    lanes = wide * slab
    per_tap, per_quarter = ch // unit, quarter // unit
    slot = part // per_quarter
    margin = (spread.shape[1] - share) // 2
    block = n_unit * slot

    load_x = [
        pltpu.make_async_copy(x_hbm.at[0, :, r], x_in.at[r], in_sem.at[2 + r]) for r in range(rows)
    ]
    load_c = [
        pltpu.make_async_copy(c_hbm.at[0, :, r], c_in.at[r], in_sem.at[2 + rows + r])
        for r in range(rows // 2)
    ]
    load_w1 = pltpu.make_async_copy(w1_hbm, w1, in_sem.at[0])
    load_w2 = pltpu.make_async_copy(w2_hbm, w2, in_sem.at[1])
    for copy in load_x + load_c:
        copy.start()
    load_w1.start()
    load_w2.start()

    barrier = pltpu.get_barrier_semaphore()

    def greet(peer):
        pl.semaphore_signal(barrier, inc=1, device_id=peer, device_id_type=MESH)

    @pl.when(tile > 0)
    def _():
        greet({"tile": tile - 1})

    @pl.when(tile < n_tile - 1)
    def _():
        greet({"tile": tile + 1})

    for i in range(1, n_dp):
        greet({"dp": lax.rem(dp + i, n_dp)})
    for j in range(1, n_z):
        greet({"tile": 2 * lax.rem(z + j, n_z) + core})

    span = 3 * ch

    def flip(src, dst):
        for tap in range(27):
            dst[tap * ch : (tap + 1) * ch, :] = src[tap * ch : (tap + 1) * ch, :].T

    if part > quarter:
        x_out[:, quarter:, :] = jnp.zeros((n_dp, part - quarter, lanes), BF16)
        hid_out[:, quarter:, :] = jnp.zeros((n_dp, part - quarter, lanes), BF16)
    lane = lax.broadcasted_iota(jnp.int32, (16, 2 * slab), 1)
    frame = lax.rem(lax.div(lane, cols), frames)
    number = jnp.zeros((16, 2 * slab), F32)
    for f in range(frames):
        number = jnp.where(frame == f, seg[0, f].astype(F32), number)
    seg_rows[dp] = number.astype(BF16)

    @pl.when(tile == 0)
    def _():
        x_halo[0] = jnp.zeros(x_halo.shape[1:], BF16)
        g_halo[0] = jnp.zeros(g_halo.shape[1:], BF16)

    @pl.when(tile == n_tile - 1)
    def _():
        x_halo[1] = jnp.zeros(x_halo.shape[1:], BF16)
        g_halo[1] = jnp.zeros(g_halo.shape[1:], BF16)

    for copy in load_x + load_c:
        copy.wait()
    beside = jnp.where(tile > 0, 1, 0) + jnp.where(tile < n_tile - 1, 1, 0)
    pl.semaphore_wait(barrier, n_dp - 1 + n_z - 1 + beside)

    g_rows = c_in.shape[0]

    def halo(side):
        peer = {"tile": tile - 1 if side == 0 else tile + 1}
        return (
            pltpu.make_async_remote_copy(
                src_ref=x_in.at[0:2] if side == 0 else x_in.at[rows - 2 : rows],
                dst_ref=x_halo.at[1 - side],
                send_sem=h_send.at[side], recv_sem=h_recv.at[1 - side],
                device_id=peer, device_id_type=MESH,
            ),
            pltpu.make_async_remote_copy(
                src_ref=c_in.at[0:1] if side == 0 else c_in.at[g_rows - 1 : g_rows],
                dst_ref=g_halo.at[1 - side],
                send_sem=h_send.at[2 + side], recv_sem=h_recv.at[2 + 1 - side],
                device_id=peer, device_id_type=MESH,
            ),
        )

    @pl.when(tile > 0)
    def _():
        for copy in halo(0):
            copy.start()

    @pl.when(tile < n_tile - 1)
    def _():
        for copy in halo(1):
            copy.start()

    def to_dp(src, dst, sends, recvs):
        return [
            pltpu.make_async_remote_copy(
                src_ref=src(lax.rem(dp + i, n_dp)), dst_ref=dst,
                send_sem=sends.at[i - 1], recv_sem=recvs.at[i - 1],
                device_id={"dp": lax.rem(dp + i, n_dp)}, device_id_type=MESH,
            )
            for i in range(1, n_dp)
        ]

    def start(copies):
        for copy in copies:
            copy.start()

    def wait(copies):
        for copy in copies:
            copy.wait()

    copies_cot = to_dp(lambda q: c_in, cot_got.at[dp], k_send, k_recv)
    copies_seg = to_dp(lambda q: seg_rows.at[dp], seg_rows.at[dp], s_send, s_recv)
    start(copies_cot)
    start(copies_seg)
    cot_got[dp] = c_in[...]

    def deal(v, out, at):
        v = v.reshape(-1, ch).T.astype(BF16)
        for q in range(n_dp):
            out[q, 0:quarter, at : at + v.shape[1]] = v[q * quarter : (q + 1) * quarter]

    mine = x_in[...].astype(F32)
    deal(mine, x_out, 0)
    copies_x = [
        to_dp(lambda q: x_out.at[q, :, 0:cells], x_got.at[dp, :, 0:cells], x_send.at[0], x_recv.at[0]),
        to_dp(lambda q: x_out.at[q, :, cells:], x_got.at[dp, :, cells:], x_send.at[1], x_recv.at[1]),
    ]
    start(copies_x[0])

    load_w1.wait()
    load_w2.wait()
    flip(w2, w2t)
    flip(w1, w1t)
    same = [None]
    for t in range(1, 3):
        same.append(
            [None] * t
            + [jnp.where(seg[0, f] == seg[0, f - t], 1.0, 0.0).astype(F32) for f in range(t, frames)]
        )

    @pl.when(tile > 0)
    def _():
        for copy in halo(0):
            copy.wait_send()
        for copy in halo(1):
            copy.wait_recv()

    @pl.when(tile < n_tile - 1)
    def _():
        for copy in halo(1):
            copy.wait_send()
        for copy in halo(0):
            copy.wait_recv()

    def four(v):
        return v.reshape(v.shape[0], frames, cols, ch)

    x_all = jnp.concatenate([x_halo[0].astype(F32), mine, x_halo[1].astype(F32)], axis=0)
    copies_hid = to_dp(lambda q: hid_out.at[q], hid_got.at[dp], t_send, t_recv)
    copies_act = to_dp(lambda q: act_got.at[dp], act_got.at[dp], g_send, g_recv)

    deal(jnp.concatenate([x_all[wide : wide + 1], x_all[1:2]], axis=0), x_out, cells)
    start(copies_x[1])
    x_got[dp] = x_out[dp]
    fill_columns(cols_x, x_all, same, False)
    c_all = jnp.concatenate([g_halo[0], c_in[...], g_halo[1]], axis=0).astype(F32) * 0.25
    half = (g_rows + 2) * slab // 2
    c_all = c_all.reshape(half, ch)
    g_tmp[pl.ds(0, half, stride=2), :] = c_all
    g_tmp[pl.ds(1, half, stride=2), :] = c_all
    g_all = g_tmp[...].reshape(g_rows + 2, slab, ch)
    g_all = jnp.stack([g_all, g_all], axis=1).reshape(2 * g_all.shape[0], slab, ch)

    first = conv_dots(cols_x, w1, 0, wide, slab, False)
    sigma = 1.0 / (1.0 + jnp.exp(-first))
    top = jnp.where(tile > 0, 1.0, 0.0).astype(F32)
    low = jnp.where(tile < n_tile - 1, 1.0, 0.0).astype(F32)

    def edges(v):
        v = v.reshape(wide, slab, ch)
        return jnp.concatenate([v[:1] * top, v[1:-1], v[-1:] * low], axis=0)

    def first_unit(to, q):
        unit_at = lax.div(share, unit) * to
        beyond = jnp.clip(lax.rem(unit_at, per_tap) - per_quarter * q, 0, per_quarter)
        return jnp.minimum(per_quarter * lax.div(unit_at, per_tap) + beyond, taps * per_quarter - n_unit)

    def window(to):
        return pl.ds(pl.multiple_of(first_unit(to, dp) * slot, 16), block)

    def copies_a(g):
        return [
            pltpu.make_async_remote_copy(
                src_ref=flat.at[g, window(2 * k + 1 - core)], dst_ref=recv_a.at[g, k],
                send_sem=a_send.at[g, k], recv_sem=a_recv.at[g, k],
                device_id={"tile": tile + 1 - 2 * core}, device_id_type=MESH,
            )
            for k in range(n_z)
        ]

    def copies_c(g):
        return [
            pltpu.make_async_remote_copy(
                src_ref=send_c.at[g, j - 1], dst_ref=recv_c.at[g, j - 1],
                send_sem=c_send.at[g, j - 1], recv_sem=c_recv.at[g, j - 1],
                device_id={"tile": 2 * lax.rem(z + j, n_z) + core}, device_id_type=MESH,
            )
            for j in range(1, n_z)
        ]

    def copies_d(g):
        return to_dp(lambda q: every.at[g, dp], every.at[g, dp], d_send.at[g], d_recv.at[g])

    def sender(i):
        return lax.rem(dp + n_dp - i, n_dp)

    def make_masks(d):
        number = seg_rows[d].astype(F32)[0:8]
        at = lax.broadcasted_iota(jnp.int32, (8, 2 * slab), 1)
        when = lax.rem(lax.div(at, cols), frames)
        col = lax.rem(at, cols)
        for t in range(3):
            keep = jnp.ones((8, 2 * slab), F32)
            if t > 0:
                keep = jnp.where(number == pltpu.roll(number, t * cols, 1), 1.0, 0.0)
                keep = jnp.where(when >= t, keep, 0.0)
            for b in range(3):
                inside = jnp.where((col + (b - 1) >= 0) & (col + (b - 1) < cols), keep, 0.0)
                mask_rows[d, t * 3 + b] = inside

    def turn(g, d, got):
        v = got[d].astype(F32)[0:part]
        for t in range(3):
            for b in range(3):
                shift = t * cols - (b - 1)
                moved = v if shift == 0 else pltpu.roll(v, shift % lanes, 1)
                if t > 0 or b != 1:
                    keep = jnp.concatenate([mask_rows[d, t * 3 + b]] * (wide // 2), axis=1)
                    moved = moved * jnp.concatenate([keep] * (part // 8), axis=0)
                for a in range(3):
                    w = moved if a == 1 else pltpu.roll(moved, (1 - a) * slab % lanes, 1)
                    at = ((t * 3 + a) * 3 + b) * part
                    turned[g, d, at : at + part, :] = w[:, 0:cells].astype(BF16)

    def partial_sum(g, d, right, fresh):
        term = jnp.dot(turned[g, d], right, preferred_element_type=F32)
        flat[g] = term if fresh else flat[g] + term

    def step_b(g):
        wait(copies_a(g))
        for k in range(n_z):
            sum_a[g, k] = flat[g, window(2 * k + core), :] + recv_a[g, k]
        for j in range(1, n_z):
            send_c[g, j - 1] = sum_a[g, lax.rem(z + j, n_z)].astype(BF16)
        start(copies_c(g))

    def step_c(g):
        wait(copies_c(g))
        total = sum_a[g, z]
        for j in range(1, n_z):
            total = total + recv_c[g, j - 1].astype(F32)
        every[g, dp] = (total * scale).astype(BF16)
        start(copies_d(g))

    def step_d(g):
        wait(copies_d(g))
        for q in range(n_dp):
            v = every[g, q].astype(F32)
            for i in range(n_unit):
                u = first_unit(tile, q) + i
                at = ch * lax.div(u, per_quarter) + unit * lax.rem(u, per_quarter) + quarter * q - share * tile
                at = pl.multiple_of(at + margin, 8)
                spread[g, pl.ds(at, unit), :] = v[i * slot : i * slot + unit]
        out_v[g] = spread[g, margin : margin + share, :]
        copy = pltpu.make_async_copy(out_v.at[g], outs[g], out_sem.at[g])
        copy.start()
        return copy

    hidden = edges(first * sigma)
    by_row = hidden.reshape(wide, slab, ch)
    deal(jnp.concatenate([by_row[1:], by_row[:1]], axis=0), hid_out, 0)
    start(copies_hid)
    hid_got[dp] = hid_out[dp]
    g_own = g_all[2 : 2 + rows].reshape(cells, ch)
    fill_columns(cols_g, four(g_all), same, True)
    hidden_grad = conv_dots(cols_g, w2t, 0, wide, slab, True)
    act = edges(hidden_grad * sigma * (1.0 + first * (1.0 - sigma)))
    act_got[dp] = act[1 : 1 + rows].reshape(cells, ch).astype(BF16)
    start(copies_act)

    wait(copies_seg)
    for d in range(n_dp):
        make_masks(d)
    wait(copies_cot)
    for d in range(n_dp):
        v = (cot_got[d].astype(F32) * 0.25).reshape(cells // 4, ch)
        g_tmp[pl.ds(0, cells // 4, stride=2), :] = v
        g_tmp[pl.ds(1, cells // 4, stride=2), :] = v
        v = g_tmp[0 : cells // 2, :].astype(BF16).reshape(rows // 2, slab, ch)
        g_got[d] = jnp.stack([v, v], axis=1).reshape(cells, ch)
    wait(copies_x[0])
    wait(copies_x[1])
    for d in range(n_dp):
        turn(0, d, x_got)
    fill_columns(cols_h, four(hidden), same, False)
    for i in range(n_dp):
        if i > 0:
            copies_hid[i - 1].wait()
        turn(1, sender(i), hid_got)
        partial_sum(1, sender(i), g_got[sender(i)], i == 0)
    start(copies_a(1))
    for i in range(n_dp):
        if i > 0:
            copies_act[i - 1].wait()
        partial_sum(0, sender(i), act_got[sender(i)], i == 0)
    start(copies_a(0))
    step_b(1)
    step_b(0)

    second = conv_dots(cols_h, w2, 0, rows, slab, False)
    summed = mine.reshape(rows, slab, ch) + second.reshape(rows, slab, ch)
    pairs = rows // 2
    for i in range(pairs):
        pool_tmp[i * slab : (i + 1) * slab, :] = summed[2 * i] + summed[2 * i + 1]
    for i in range(pairs):
        for f in range(frames):
            at = i * slab + f * cols
            pooled[f, i] = 0.25 * (
                pool_tmp[pl.ds(at, cols // 2, stride=2), :]
                + pool_tmp[pl.ds(at + 1, cols // 2, stride=2), :]
            )
    put_pooled = pltpu.make_async_copy(pooled, pooled_hbm.at[0], out_sem.at[2])
    put_pooled.start()
    fill_columns(cols_a, four(act), same, True)
    back = conv_dots(cols_a, w1t, 0, rows, slab, True)
    total = (g_own + back).reshape(rows, frames, cols, ch)
    for r in range(rows):
        in_grad[:, r] = total[r]
    put_grad = pltpu.make_async_copy(in_grad, in_grad_hbm.at[0], out_sem.at[3])
    put_grad.start()
    step_c(1)
    step_c(0)
    puts = [put_pooled, put_grad, step_d(1), step_d(0)]
    for copy in puts:
        copy.wait()


def hand_out(*refs):
    held, load_sem, store_sem = refs[8:12], refs[12], refs[13]
    loads = [pltpu.make_async_copy(refs[i], held[i], load_sem.at[i]) for i in range(4)]
    stores = [pltpu.make_async_copy(held[i], refs[4 + i], store_sem.at[i]) for i in range(4)]
    for copy in loads:
        copy.start()
    for i in (0, 2, 3, 1):
        loads[i].wait()
        stores[i].start()
    for copy in stores:
        copy.wait()


def local(n_tile, n_dp, clip_frames, segments, weight_first, weight_second, cotangent):
    _, frames, rows, cols, ch = clip_frames.shape
    slab = frames * cols
    taps = weight_first.shape[0]
    share = taps // n_tile
    n_z = n_tile // 2
    quarter = ch // n_dp
    part = up16(quarter)
    unit = math.gcd(share, quarter)
    per_quarter = quarter // unit

    def before(to, q):
        whole, rest = divmod(share // unit * to, ch // unit)
        return per_quarter * whole + min(max(rest - per_quarter * q, 0), per_quarter)

    n_unit = max(before(k + 1, q) - before(k, q) for k in range(n_tile) for q in range(n_dp))
    block = n_unit * (part // per_quarter)
    span = share + 2 * ch * (n_unit // per_quarter + 2)
    scale = 1.0 / math.sqrt(n_dp * n_tile * rows * slab)
    vmem = pl.BlockSpec(memory_space=pltpu.VMEM)
    cells = rows * slab
    lanes = (rows + 2) * slab
    sem = pltpu.SemaphoreType.DMA
    anywhere = pl.BlockSpec(memory_space=pltpu.HBM)
    shapes = (
        jax.ShapeDtypeStruct((1, frames, rows // 2, cols // 2, ch), F32),
        jax.ShapeDtypeStruct((1, frames, rows, cols, ch), F32),
        jax.ShapeDtypeStruct((share, ch), F32),
        jax.ShapeDtypeStruct((share, ch), F32),
    )
    results = pl.pallas_call(
        functools.partial(kernel, (n_tile, n_dp, share, quarter, part, unit, n_unit, scale)),
        out_shape=shapes,
        in_specs=[pl.BlockSpec(memory_space=pltpu.SMEM)] + [anywhere] * 4,
        out_specs=(anywhere,) * 4,
        scratch_shapes=[
            pltpu.VMEM((frames, rows // 2, cols // 2, ch), F32),
            pltpu.VMEM((frames, rows, cols, ch), F32),
            sem((4,)),
            pltpu.VMEM((rows, frames, cols, ch), BF16),
            pltpu.VMEM((taps, ch), BF16),
            pltpu.VMEM((taps, ch), BF16),
            pltpu.VMEM((rows // 2, frames, cols // 2, ch), BF16),
            pltpu.VMEM(((rows // 2 + 2) * slab, ch), F32),
            sem((2 + rows + rows // 2,)),
            pltpu.VMEM((2, 2, frames, cols, ch), BF16),
            pltpu.VMEM((2, 1, frames, cols // 2, ch), BF16),
            pltpu.VMEM(((rows + 4) * slab, 9 * ch), BF16),
            pltpu.VMEM(((rows + 2) * slab, 9 * ch), BF16),
            pltpu.VMEM(((rows + 4) * slab, 9 * ch), BF16),
            pltpu.VMEM(((rows + 2) * slab, 9 * ch), BF16),
            pltpu.VMEM((taps, ch), BF16),
            pltpu.VMEM((taps, ch), BF16),
            pltpu.VMEM((cells // 2, ch), F32),
            pltpu.VMEM((n_dp, 16, 2 * slab), BF16),
            pltpu.VMEM((n_dp, 9, 8, 2 * slab), F32),
            pltpu.VMEM((n_dp, part, lanes), BF16),
            pltpu.VMEM((n_dp, part, lanes), BF16),
            pltpu.VMEM((n_dp, part, lanes), BF16),
            pltpu.VMEM((n_dp, part, lanes), BF16),
            pltpu.VMEM((n_dp, rows // 2, frames, cols // 2, ch), BF16),
            pltpu.VMEM((n_dp, cells, ch), BF16),
            pltpu.VMEM((n_dp, cells, ch), BF16),
            pltpu.VMEM((2, n_dp, taps // ch * part, cells), BF16),
            pltpu.VMEM((2, taps // ch * part, ch), F32),
            pltpu.VMEM((2, n_z, block, ch), F32),
            pltpu.VMEM((2, n_z, block, ch), F32),
            pltpu.VMEM((2, n_z - 1, block, ch), BF16),
            pltpu.VMEM((2, n_z - 1, block, ch), BF16),
            pltpu.VMEM((2, n_dp, block, ch), BF16),
            pltpu.VMEM((2, span, ch), F32),
            pltpu.VMEM((2, share, ch), F32),
            sem((4,)), sem((4,)),
            sem((2, n_dp - 1)), sem((2, n_dp - 1)),
            sem((n_dp - 1,)), sem((n_dp - 1,)),
            sem((n_dp - 1,)), sem((n_dp - 1,)),
            sem((n_dp - 1,)), sem((n_dp - 1,)),
            sem((n_dp - 1,)), sem((n_dp - 1,)),
            sem((2, n_z)), sem((2, n_z)),
            sem((2, n_z - 1)), sem((2, n_z - 1)),
            sem((2, n_dp - 1)), sem((2, n_dp - 1)),
        ],
        compiler_params=pltpu.CompilerParams(
            collective_id=0, has_side_effects=True, vmem_limit_bytes=60 * 1024 * 1024
        ),
    )(segments, clip_frames, weight_first, weight_second, cotangent)
    return tuple(
        pl.pallas_call(
            hand_out,
            out_shape=shapes,
            in_specs=[pl.BlockSpec(memory_space=pl.ANY)] * 4,
            out_specs=(pl.BlockSpec(memory_space=pl.ANY),) * 4,
            scratch_shapes=[pltpu.VMEM(v.shape, v.dtype) for v in shapes] + [sem((4,))] * 2,
        )(*results)
    )


def solution(mesh):
    return jax.shard_map(
        functools.partial(local, mesh.shape["tile"], mesh.shape["dp"]),
        mesh=mesh,
        in_specs=(
            P("dp", None, "tile", None, None),
            P("dp", None),
            P(),
            P(),
            P("dp", None, "tile", None, None),
        ),
        out_specs=(
            P("dp", None, "tile", None, None),
            P("dp", None, "tile", None, None),
            P("tile", None),
            P("tile", None),
        ),
        check_vma=False,
    )
```

```python
import functools
import math

import jax
import jax.numpy as jnp
from jax import lax
from jax.experimental import pallas as pl
from jax.experimental.pallas import tpu as pltpu
from jax.sharding import PartitionSpec as P

MESH = pl.DeviceIdType.MESH
F32 = jnp.float32
BF16 = jnp.bfloat16


def up16(n):
    return -(-n // 16) * 16


def shifted_cols(cells, step):
    if step == 0:
        return cells
    cols = cells.shape[2]
    col = lax.broadcasted_iota(jnp.int32, cells.shape, 2)
    moved = pltpu.roll(cells, (-step) % cols, 2)
    keep = (col < cols - 1) if step == 1 else (col > 0)
    return jnp.where(keep, moved, 0.0)


def fill_columns(dst, cells, same, reverse):
    rows, frames, cols, ch = cells.shape
    for ci in range(3):
        moved = shifted_cols(cells, (1 - ci) if reverse else (ci - 1))
        for t in range(3):
            zero = jnp.zeros((rows, cols, ch), F32)
            parts = []
            for f in range(frames):
                src = f + t if reverse else f - t
                if src < 0 or src >= frames:
                    parts.append(zero)
                elif t == 0:
                    parts.append(moved[:, src])
                else:
                    parts.append(moved[:, src] * same[t][max(f, src)])
            block = jnp.stack(parts, axis=1).reshape(rows * frames * cols, ch)
            at = (t * 3 + ci) * ch
            dst[:, at : at + ch] = block.astype(BF16)


def conv_dots(cols_ref, w_ref, start, rows, slab, reverse):
    acc = None
    span = w_ref.shape[1] * 3
    for t in range(3):
        for a in range(3):
            at = (start + (2 - a if reverse else a)) * slab
            term = jnp.dot(
                cols_ref[at : at + rows * slab, t * span : (t + 1) * span],
                w_ref[(t * 3 + a) * span : (t * 3 + a + 1) * span, :],
                preferred_element_type=F32,
            )
            acc = term if acc is None else acc + term
    return acc


def kernel(
    cfg,
    seg, x_hbm, w1_hbm, w2_hbm, c_hbm,
    pooled, in_grad, out1, out2,
    x_in, w1, w2, c_in, g_tmp, in_sem, x_halo, g_halo, cols_x, cols_h, cols_g, cols_a, w1t, w2t, pool_tmp,
    seg_rows, mask_rows, x_out, x_got, hid_out, hid_got, cot_got, act_got, g_got, turned, flat,
    recv_a, sum_a, send_c, recv_c, every, spread,
    h_send, h_recv, x_send, x_recv, s_send, s_recv, k_send, k_recv, g_send, g_recv, t_send, t_recv,
    a_send, a_recv, c_send, c_recv, d_send, d_recv,
):
    n_tile, n_dp, share, quarter, part, unit, n_unit, scale = cfg
    n_z = n_tile // 2
    rows, frames, cols, ch = x_in.shape
    slab = frames * cols
    tile = lax.axis_index("tile")
    dp = lax.axis_index("dp")
    core = lax.rem(tile, 2)
    z = lax.div(tile, 2)
    taps = w1.shape[0] // ch
    outs = (out1, out2)
    wide = rows + 2
    cells = rows * slab
    lanes = wide * slab
    per_tap, per_quarter = ch // unit, quarter // unit
    slot = part // per_quarter
    margin = (spread.shape[1] - share) // 2
    block = n_unit * slot

    load_x = [
        pltpu.make_async_copy(x_hbm.at[0, :, r], x_in.at[r], in_sem.at[2 + r]) for r in range(rows)
    ]
    load_c = [
        pltpu.make_async_copy(c_hbm.at[0, :, r], c_in.at[r], in_sem.at[2 + rows + r])
        for r in range(rows // 2)
    ]
    load_w1 = pltpu.make_async_copy(w1_hbm, w1, in_sem.at[0])
    load_w2 = pltpu.make_async_copy(w2_hbm, w2, in_sem.at[1])
    for copy in load_x + load_c:
        copy.start()
    load_w1.start()
    load_w2.start()

    barrier = pltpu.get_barrier_semaphore()

    def greet(peer):
        pl.semaphore_signal(barrier, inc=1, device_id=peer, device_id_type=MESH)

    @pl.when(tile > 0)
    def _():
        greet({"tile": tile - 1})

    @pl.when(tile < n_tile - 1)
    def _():
        greet({"tile": tile + 1})

    for i in range(1, n_dp):
        greet({"dp": lax.rem(dp + i, n_dp)})
    for j in range(1, n_z):
        greet({"tile": 2 * lax.rem(z + j, n_z) + core})

    span = 3 * ch

    def flip(src, dst):
        for tap in range(27):
            dst[tap * ch : (tap + 1) * ch, :] = src[tap * ch : (tap + 1) * ch, :].T

    if part > quarter:
        x_out[:, quarter:, :] = jnp.zeros((n_dp, part - quarter, lanes), BF16)
        hid_out[:, quarter:, :] = jnp.zeros((n_dp, part - quarter, lanes), BF16)
    lane = lax.broadcasted_iota(jnp.int32, (16, 2 * slab), 1)
    frame = lax.rem(lax.div(lane, cols), frames)
    number = jnp.zeros((16, 2 * slab), F32)
    for f in range(frames):
        number = jnp.where(frame == f, seg[0, f].astype(F32), number)
    seg_rows[dp] = number.astype(BF16)

    @pl.when(tile == 0)
    def _():
        x_halo[0] = jnp.zeros(x_halo.shape[1:], BF16)
        g_halo[0] = jnp.zeros(g_halo.shape[1:], BF16)

    @pl.when(tile == n_tile - 1)
    def _():
        x_halo[1] = jnp.zeros(x_halo.shape[1:], BF16)
        g_halo[1] = jnp.zeros(g_halo.shape[1:], BF16)

    for copy in load_x + load_c:
        copy.wait()
    beside = jnp.where(tile > 0, 1, 0) + jnp.where(tile < n_tile - 1, 1, 0)
    pl.semaphore_wait(barrier, n_dp - 1 + n_z - 1 + beside)

    g_rows = c_in.shape[0]

    def halo(side):
        peer = {"tile": tile - 1 if side == 0 else tile + 1}
        return (
            pltpu.make_async_remote_copy(
                src_ref=x_in.at[0:2] if side == 0 else x_in.at[rows - 2 : rows],
                dst_ref=x_halo.at[1 - side],
                send_sem=h_send.at[side], recv_sem=h_recv.at[1 - side],
                device_id=peer, device_id_type=MESH,
            ),
            pltpu.make_async_remote_copy(
                src_ref=c_in.at[0:1] if side == 0 else c_in.at[g_rows - 1 : g_rows],
                dst_ref=g_halo.at[1 - side],
                send_sem=h_send.at[2 + side], recv_sem=h_recv.at[2 + 1 - side],
                device_id=peer, device_id_type=MESH,
            ),
        )

    @pl.when(tile > 0)
    def _():
        for copy in halo(0):
            copy.start()

    @pl.when(tile < n_tile - 1)
    def _():
        for copy in halo(1):
            copy.start()

    def to_dp(src, dst, sends, recvs):
        return [
            pltpu.make_async_remote_copy(
                src_ref=src(lax.rem(dp + i, n_dp)), dst_ref=dst,
                send_sem=sends.at[i - 1], recv_sem=recvs.at[i - 1],
                device_id={"dp": lax.rem(dp + i, n_dp)}, device_id_type=MESH,
            )
            for i in range(1, n_dp)
        ]

    def start(copies):
        for copy in copies:
            copy.start()

    def wait(copies):
        for copy in copies:
            copy.wait()

    copies_cot = to_dp(lambda q: c_in, cot_got.at[dp], k_send, k_recv)
    copies_seg = to_dp(lambda q: seg_rows.at[dp], seg_rows.at[dp], s_send, s_recv)
    start(copies_cot)
    start(copies_seg)
    cot_got[dp] = c_in[...]

    def deal(v, out, at):
        v = v.reshape(-1, ch).T.astype(BF16)
        for q in range(n_dp):
            out[q, 0:quarter, at : at + v.shape[1]] = v[q * quarter : (q + 1) * quarter]

    mine = x_in[...].astype(F32)
    deal(mine, x_out, 0)
    copies_x = [
        to_dp(lambda q: x_out.at[q, :, 0:cells], x_got.at[dp, :, 0:cells], x_send.at[0], x_recv.at[0]),
        to_dp(lambda q: x_out.at[q, :, cells:], x_got.at[dp, :, cells:], x_send.at[1], x_recv.at[1]),
    ]
    start(copies_x[0])

    load_w1.wait()
    load_w2.wait()
    flip(w2, w2t)
    flip(w1, w1t)
    same = [None]
    for t in range(1, 3):
        same.append(
            [None] * t
            + [jnp.where(seg[0, f] == seg[0, f - t], 1.0, 0.0).astype(F32) for f in range(t, frames)]
        )

    @pl.when(tile > 0)
    def _():
        for copy in halo(0):
            copy.wait_send()
        for copy in halo(1):
            copy.wait_recv()

    @pl.when(tile < n_tile - 1)
    def _():
        for copy in halo(1):
            copy.wait_send()
        for copy in halo(0):
            copy.wait_recv()

    def four(v):
        return v.reshape(v.shape[0], frames, cols, ch)

    x_all = jnp.concatenate([x_halo[0].astype(F32), mine, x_halo[1].astype(F32)], axis=0)
    copies_hid = to_dp(lambda q: hid_out.at[q], hid_got.at[dp], t_send, t_recv)
    copies_act = to_dp(lambda q: act_got.at[dp], act_got.at[dp], g_send, g_recv)

    deal(jnp.concatenate([x_all[wide : wide + 1], x_all[1:2]], axis=0), x_out, cells)
    start(copies_x[1])
    x_got[dp] = x_out[dp]
    fill_columns(cols_x, x_all, same, False)
    c_all = jnp.concatenate([g_halo[0], c_in[...], g_halo[1]], axis=0).astype(F32) * 0.25
    half = (g_rows + 2) * slab // 2
    c_all = c_all.reshape(half, ch)
    g_tmp[pl.ds(0, half, stride=2), :] = c_all
    g_tmp[pl.ds(1, half, stride=2), :] = c_all
    g_all = g_tmp[...].reshape(g_rows + 2, slab, ch)
    g_all = jnp.stack([g_all, g_all], axis=1).reshape(2 * g_all.shape[0], slab, ch)

    first = conv_dots(cols_x, w1, 0, wide, slab, False)
    sigma = 1.0 / (1.0 + jnp.exp(-first))
    top = jnp.where(tile > 0, 1.0, 0.0).astype(F32)
    low = jnp.where(tile < n_tile - 1, 1.0, 0.0).astype(F32)

    def edges(v):
        v = v.reshape(wide, slab, ch)
        return jnp.concatenate([v[:1] * top, v[1:-1], v[-1:] * low], axis=0)

    def first_unit(to, q):
        unit_at = lax.div(share, unit) * to
        beyond = jnp.clip(lax.rem(unit_at, per_tap) - per_quarter * q, 0, per_quarter)
        return jnp.minimum(per_quarter * lax.div(unit_at, per_tap) + beyond, taps * per_quarter - n_unit)

    def window(to):
        return pl.ds(pl.multiple_of(first_unit(to, dp) * slot, 16), block)

    def copies_a(g):
        return [
            pltpu.make_async_remote_copy(
                src_ref=flat.at[g, window(2 * k + 1 - core)], dst_ref=recv_a.at[g, k],
                send_sem=a_send.at[g, k], recv_sem=a_recv.at[g, k],
                device_id={"tile": tile + 1 - 2 * core}, device_id_type=MESH,
            )
            for k in range(n_z)
        ]

    def copies_c(g):
        return [
            pltpu.make_async_remote_copy(
                src_ref=send_c.at[g, j - 1], dst_ref=recv_c.at[g, j - 1],
                send_sem=c_send.at[g, j - 1], recv_sem=c_recv.at[g, j - 1],
                device_id={"tile": 2 * lax.rem(z + j, n_z) + core}, device_id_type=MESH,
            )
            for j in range(1, n_z)
        ]

    def copies_d(g):
        return to_dp(lambda q: every.at[g, dp], every.at[g, dp], d_send.at[g], d_recv.at[g])

    def sender(i):
        return lax.rem(dp + n_dp - i, n_dp)

    def make_masks(d):
        number = seg_rows[d].astype(F32)[0:8]
        at = lax.broadcasted_iota(jnp.int32, (8, 2 * slab), 1)
        when = lax.rem(lax.div(at, cols), frames)
        col = lax.rem(at, cols)
        for t in range(3):
            keep = jnp.ones((8, 2 * slab), F32)
            if t > 0:
                keep = jnp.where(number == pltpu.roll(number, t * cols, 1), 1.0, 0.0)
                keep = jnp.where(when >= t, keep, 0.0)
            for b in range(3):
                inside = jnp.where((col + (b - 1) >= 0) & (col + (b - 1) < cols), keep, 0.0)
                mask_rows[d, t * 3 + b] = inside

    def turn(g, d, got):
        v = got[d].astype(F32)[0:part]
        for t in range(3):
            for b in range(3):
                shift = t * cols - (b - 1)
                moved = v if shift == 0 else pltpu.roll(v, shift % lanes, 1)
                if t > 0 or b != 1:
                    keep = jnp.concatenate([mask_rows[d, t * 3 + b]] * (wide // 2), axis=1)
                    moved = moved * jnp.concatenate([keep] * (part // 8), axis=0)
                for a in range(3):
                    w = moved if a == 1 else pltpu.roll(moved, (1 - a) * slab % lanes, 1)
                    at = ((t * 3 + a) * 3 + b) * part
                    turned[g, d, at : at + part, :] = w[:, 0:cells].astype(BF16)

    def partial_sum(g, d, right, fresh):
        term = jnp.dot(turned[g, d], right, preferred_element_type=F32)
        flat[g] = term if fresh else flat[g] + term

    def step_b(g):
        wait(copies_a(g))
        for k in range(n_z):
            sum_a[g, k] = flat[g, window(2 * k + core), :] + recv_a[g, k]
        for j in range(1, n_z):
            send_c[g, j - 1] = sum_a[g, lax.rem(z + j, n_z)].astype(BF16)
        start(copies_c(g))

    def step_c(g):
        wait(copies_c(g))
        total = sum_a[g, z]
        for j in range(1, n_z):
            total = total + recv_c[g, j - 1].astype(F32)
        every[g, dp] = (total * scale).astype(BF16)
        start(copies_d(g))

    def step_d(g):
        wait(copies_d(g))
        for q in range(n_dp):
            v = every[g, q].astype(F32)
            for i in range(n_unit):
                u = first_unit(tile, q) + i
                at = ch * lax.div(u, per_quarter) + unit * lax.rem(u, per_quarter) + quarter * q - share * tile
                at = pl.multiple_of(at + margin, 8)
                spread[g, pl.ds(at, unit), :] = v[i * slot : i * slot + unit]
        outs[g][...] = spread[g, margin : margin + share, :]

    hidden = edges(first * sigma)
    by_row = hidden.reshape(wide, slab, ch)
    deal(jnp.concatenate([by_row[1:], by_row[:1]], axis=0), hid_out, 0)
    start(copies_hid)
    hid_got[dp] = hid_out[dp]
    g_own = g_all[2 : 2 + rows].reshape(cells, ch)
    fill_columns(cols_g, four(g_all), same, True)
    hidden_grad = conv_dots(cols_g, w2t, 0, wide, slab, True)
    act = edges(hidden_grad * sigma * (1.0 + first * (1.0 - sigma)))
    act_got[dp] = act[1 : 1 + rows].reshape(cells, ch).astype(BF16)
    start(copies_act)

    wait(copies_seg)
    for d in range(n_dp):
        make_masks(d)
    wait(copies_cot)
    for d in range(n_dp):
        v = (cot_got[d].astype(F32) * 0.25).reshape(cells // 4, ch)
        g_tmp[pl.ds(0, cells // 4, stride=2), :] = v
        g_tmp[pl.ds(1, cells // 4, stride=2), :] = v
        v = g_tmp[0 : cells // 2, :].astype(BF16).reshape(rows // 2, slab, ch)
        g_got[d] = jnp.stack([v, v], axis=1).reshape(cells, ch)
    wait(copies_x[0])
    wait(copies_x[1])
    for d in range(n_dp):
        turn(0, d, x_got)
    fill_columns(cols_h, four(hidden), same, False)
    for i in range(n_dp):
        if i > 0:
            copies_hid[i - 1].wait()
        turn(1, sender(i), hid_got)
        partial_sum(1, sender(i), g_got[sender(i)], i == 0)
    start(copies_a(1))
    for i in range(n_dp):
        if i > 0:
            copies_act[i - 1].wait()
        partial_sum(0, sender(i), act_got[sender(i)], i == 0)
    start(copies_a(0))
    step_b(1)
    step_b(0)

    second = conv_dots(cols_h, w2, 0, rows, slab, False)
    summed = mine.reshape(rows, slab, ch) + second.reshape(rows, slab, ch)
    pairs = rows // 2
    for i in range(pairs):
        pool_tmp[i * slab : (i + 1) * slab, :] = summed[2 * i] + summed[2 * i + 1]
    for i in range(pairs):
        for f in range(frames):
            at = i * slab + f * cols
            pooled[0, f, i] = 0.25 * (
                pool_tmp[pl.ds(at, cols // 2, stride=2), :]
                + pool_tmp[pl.ds(at + 1, cols // 2, stride=2), :]
            )
    fill_columns(cols_a, four(act), same, True)
    back = conv_dots(cols_a, w1t, 0, rows, slab, True)
    total = (g_own + back).reshape(rows, frames, cols, ch)
    for r in range(rows):
        in_grad[0, :, r] = total[r]
    step_c(1)
    step_c(0)
    step_d(1)
    step_d(0)


def hand_out(*refs):
    sems = refs[8]
    copies = [pltpu.make_async_copy(refs[i], refs[4 + i], sems.at[i]) for i in (1, 2, 3, 0)]
    for copy in copies:
        copy.start()
    for copy in copies:
        copy.wait()


def local(n_tile, n_dp, clip_frames, segments, weight_first, weight_second, cotangent):
    _, frames, rows, cols, ch = clip_frames.shape
    slab = frames * cols
    taps = weight_first.shape[0]
    share = taps // n_tile
    n_z = n_tile // 2
    quarter = ch // n_dp
    part = up16(quarter)
    unit = math.gcd(share, quarter)
    per_quarter = quarter // unit

    def before(to, q):
        whole, rest = divmod(share // unit * to, ch // unit)
        return per_quarter * whole + min(max(rest - per_quarter * q, 0), per_quarter)

    n_unit = max(before(k + 1, q) - before(k, q) for k in range(n_tile) for q in range(n_dp))
    block = n_unit * (part // per_quarter)
    span = share + 2 * ch * (n_unit // per_quarter + 2)
    scale = 1.0 / math.sqrt(n_dp * n_tile * rows * slab)
    vmem = pl.BlockSpec(memory_space=pltpu.VMEM)
    cells = rows * slab
    lanes = (rows + 2) * slab
    sem = pltpu.SemaphoreType.DMA
    anywhere = pl.BlockSpec(memory_space=pltpu.HBM)
    shapes = (
        jax.ShapeDtypeStruct((1, frames, rows // 2, cols // 2, ch), F32),
        jax.ShapeDtypeStruct((1, frames, rows, cols, ch), F32),
        jax.ShapeDtypeStruct((share, ch), F32),
        jax.ShapeDtypeStruct((share, ch), F32),
    )
    held = [
        pltpu.with_memory_space_constraint(v, pltpu.HBM)
        for v in (segments, clip_frames, weight_first, weight_second, cotangent)
    ]
    results = pl.pallas_call(
        functools.partial(kernel, (n_tile, n_dp, share, quarter, part, unit, n_unit, scale)),
        out_shape=shapes,
        in_specs=[pl.BlockSpec(memory_space=pltpu.SMEM)] + [anywhere] * 4,
        out_specs=(vmem,) * 4,
        scratch_shapes=[
            pltpu.VMEM((rows, frames, cols, ch), BF16),
            pltpu.VMEM((taps, ch), BF16),
            pltpu.VMEM((taps, ch), BF16),
            pltpu.VMEM((rows // 2, frames, cols // 2, ch), BF16),
            pltpu.VMEM(((rows // 2 + 2) * slab, ch), F32),
            sem((2 + rows + rows // 2,)),
            pltpu.VMEM((2, 2, frames, cols, ch), BF16),
            pltpu.VMEM((2, 1, frames, cols // 2, ch), BF16),
            pltpu.VMEM(((rows + 4) * slab, 9 * ch), BF16),
            pltpu.VMEM(((rows + 2) * slab, 9 * ch), BF16),
            pltpu.VMEM(((rows + 4) * slab, 9 * ch), BF16),
            pltpu.VMEM(((rows + 2) * slab, 9 * ch), BF16),
            pltpu.VMEM((taps, ch), BF16),
            pltpu.VMEM((taps, ch), BF16),
            pltpu.VMEM((cells // 2, ch), F32),
            pltpu.VMEM((n_dp, 16, 2 * slab), BF16),
            pltpu.VMEM((n_dp, 9, 8, 2 * slab), F32),
            pltpu.VMEM((n_dp, part, lanes), BF16),
            pltpu.VMEM((n_dp, part, lanes), BF16),
            pltpu.VMEM((n_dp, part, lanes), BF16),
            pltpu.VMEM((n_dp, part, lanes), BF16),
            pltpu.VMEM((n_dp, rows // 2, frames, cols // 2, ch), BF16),
            pltpu.VMEM((n_dp, cells, ch), BF16),
            pltpu.VMEM((n_dp, cells, ch), BF16),
            pltpu.VMEM((2, n_dp, taps // ch * part, cells), BF16),
            pltpu.VMEM((2, taps // ch * part, ch), F32),
            pltpu.VMEM((2, n_z, block, ch), F32),
            pltpu.VMEM((2, n_z, block, ch), F32),
            pltpu.VMEM((2, n_z - 1, block, ch), BF16),
            pltpu.VMEM((2, n_z - 1, block, ch), BF16),
            pltpu.VMEM((2, n_dp, block, ch), BF16),
            pltpu.VMEM((2, span, ch), F32),
            sem((4,)), sem((4,)),
            sem((2, n_dp - 1)), sem((2, n_dp - 1)),
            sem((n_dp - 1,)), sem((n_dp - 1,)),
            sem((n_dp - 1,)), sem((n_dp - 1,)),
            sem((n_dp - 1,)), sem((n_dp - 1,)),
            sem((n_dp - 1,)), sem((n_dp - 1,)),
            sem((2, n_z)), sem((2, n_z)),
            sem((2, n_z - 1)), sem((2, n_z - 1)),
            sem((2, n_dp - 1)), sem((2, n_dp - 1)),
        ],
        compiler_params=pltpu.CompilerParams(
            collective_id=0, has_side_effects=True, vmem_limit_bytes=50 * 1024 * 1024
        ),
    )(*held)
    return tuple(
        pl.pallas_call(
            hand_out,
            out_shape=shapes,
            in_specs=[pl.BlockSpec(memory_space=pl.ANY)] * 4,
            out_specs=(pl.BlockSpec(memory_space=pl.ANY),) * 4,
            scratch_shapes=[sem((4,))],
            compiler_params=pltpu.CompilerParams(vmem_limit_bytes=4 * 1024 * 1024),
        )(*results)
    )


def solution(mesh):
    return jax.shard_map(
        functools.partial(local, mesh.shape["tile"], mesh.shape["dp"]),
        mesh=mesh,
        in_specs=(
            P("dp", None, "tile", None, None),
            P("dp", None),
            P(),
            P(),
            P("dp", None, "tile", None, None),
        ),
        out_specs=(
            P("dp", None, "tile", None, None),
            P("dp", None, "tile", None, None),
            P("tile", None),
            P("tile", None),
        ),
        check_vma=False,
    )
```

```python
import functools
import math

import jax
import jax.numpy as jnp
from jax import lax
from jax.experimental import pallas as pl
from jax.experimental.pallas import tpu as pltpu
from jax.sharding import PartitionSpec as P

MESH = pl.DeviceIdType.MESH
F32 = jnp.float32
BF16 = jnp.bfloat16


def up16(n):
    return -(-n // 16) * 16


def shifted_cols(cells, step):
    if step == 0:
        return cells
    cols = cells.shape[2]
    col = lax.broadcasted_iota(jnp.int32, cells.shape, 2)
    moved = pltpu.roll(cells, (-step) % cols, 2)
    keep = (col < cols - 1) if step == 1 else (col > 0)
    return jnp.where(keep, moved, 0.0)


def fill_columns(dst, cells, same, reverse, first=0):
    rows, frames, cols, ch = cells.shape
    for ci in range(3):
        moved = shifted_cols(cells, (1 - ci) if reverse else (ci - 1))
        for t in range(3):
            zero = jnp.zeros((rows, cols, ch), F32)
            parts = []
            for f in range(frames):
                src = f + t if reverse else f - t
                if src < 0 or src >= frames:
                    parts.append(zero)
                elif t == 0:
                    parts.append(moved[:, src])
                else:
                    parts.append(moved[:, src] * same[t][max(f, src)])
            block = jnp.stack(parts, axis=1).reshape(rows * frames * cols, ch)
            at = (t * 3 + ci) * ch
            from_row = first * frames * cols
            dst[from_row : from_row + rows * frames * cols, at : at + ch] = block.astype(BF16)


def conv_dots(cols_ref, w_ref, start, rows, slab, reverse):
    acc = None
    span = w_ref.shape[1] * 3
    for t in range(3):
        for a in range(3):
            at = (start + (2 - a if reverse else a)) * slab
            term = jnp.dot(
                cols_ref[at : at + rows * slab, t * span : (t + 1) * span],
                w_ref[(t * 3 + a) * span : (t * 3 + a + 1) * span, :],
                preferred_element_type=F32,
            )
            acc = term if acc is None else acc + term
    return acc


def own_dots(cols_ref, w_ref, rows, slab, reverse):
    total = None
    span = w_ref.shape[1] * 3
    for a in range(3):
        e = 2 - a if reverse else a
        term = None
        for t in range(3):
            one = jnp.dot(
                cols_ref[2 * slab : (2 + rows) * slab, t * span : (t + 1) * span],
                w_ref[(t * 3 + a) * span : (t * 3 + a + 1) * span, :],
                preferred_element_type=F32,
            )
            term = one if term is None else term + one
        ends = [jnp.zeros((n * slab, w_ref.shape[1]), F32) for n in (2 - e, e)]
        parts = [v for v in (ends[0], term, ends[1]) if v.shape[0] > 0]
        padded = jnp.concatenate(parts, axis=0)
        total = padded if total is None else total + padded
    return total


def edge_dots(cols_ref, w_ref, rows, slab, reverse):
    terms = []
    span = w_ref.shape[1] * 3
    for e in range(3):
        a = 2 - e if reverse else e
        term = None
        for t in range(3):
            at = slice(t * span, (t + 1) * span)
            if e == 0:
                left = cols_ref[0 : 2 * slab, at]
            elif e == 1:
                left = jnp.concatenate(
                    [cols_ref[slab : 2 * slab, at], cols_ref[(rows + 2) * slab : (rows + 3) * slab, at]], axis=0
                )
            else:
                left = cols_ref[(rows + 2) * slab : (rows + 4) * slab, at]
            one = jnp.dot(
                left, w_ref[(t * 3 + a) * span : (t * 3 + a + 1) * span, :], preferred_element_type=F32
            )
            term = one if term is None else term + one
        terms.append(term)
    return jnp.concatenate(
        [
            terms[0][:slab] + terms[1][:slab],
            terms[0][slab:],
            jnp.zeros(((rows - 2) * slab, w_ref.shape[1]), F32),
            terms[2][:slab],
            terms[2][slab:] + terms[1][slab:],
        ],
        axis=0,
    )


def kernel(
    cfg,
    seg, x_hbm, w1_hbm, w2_hbm, c_hbm,
    pooled, in_grad, out1, out2,
    x_in, w1, w2, c_in, g_tmp, in_sem, x_halo, g_halo, cols_x, cols_h, cols_g, cols_a, w1t, w2t, pool_tmp,
    own_x, own_g, mask_rows, c_flat, early_out, early_got, late_out, late_got, act_got, g_got, turned, flat,
    recv_a, sum_a, send_c, recv_c, every, spread,
    h_send, h_recv, x_send, x_recv, g_send, g_recv, t_send, t_recv,
    a_send, a_recv, c_send, c_recv, d_send, d_recv,
):
    n_tile, n_dp, share, quarter, part, unit, n_unit, scale = cfg
    n_z = n_tile // 2
    rows, frames, cols, ch = x_in.shape
    slab = frames * cols
    tile = lax.axis_index("tile")
    dp = lax.axis_index("dp")
    core = lax.rem(tile, 2)
    z = lax.div(tile, 2)
    taps = w1.shape[0] // ch
    outs = (out1, out2)
    wide = rows + 2
    cells = rows * slab
    lanes = wide * slab
    per_tap, per_quarter = ch // unit, quarter // unit
    slot = part // per_quarter
    own_lanes = cells // ch
    cot_at = own_lanes * part
    seg_at = cot_at + cells // 4
    edge_at = (own_lanes + 1) * part
    margin = (spread.shape[1] - share) // 2
    block = n_unit * slot

    load_x = [
        pltpu.make_async_copy(x_hbm.at[0, :, r], x_in.at[r], in_sem.at[2 + r]) for r in range(rows)
    ]
    load_c = [
        pltpu.make_async_copy(c_hbm.at[0, :, r], c_in.at[r], in_sem.at[2 + rows + r])
        for r in range(rows // 2)
    ]
    load_w1 = pltpu.make_async_copy(w1_hbm, w1, in_sem.at[0])
    load_w2 = pltpu.make_async_copy(w2_hbm, w2, in_sem.at[1])
    for copy in load_x + load_c:
        copy.start()
    load_w1.start()
    load_w2.start()

    barrier = pltpu.get_barrier_semaphore()

    def greet(peer):
        pl.semaphore_signal(barrier, inc=1, device_id=peer, device_id_type=MESH)

    @pl.when(tile > 0)
    def _():
        greet({"tile": tile - 1})

    @pl.when(tile < n_tile - 1)
    def _():
        greet({"tile": tile + 1})

    for i in range(1, n_dp):
        greet({"dp": lax.rem(dp + i, n_dp)})
    for j in range(1, n_z):
        greet({"tile": 2 * lax.rem(z + j, n_z) + core})

    span = 3 * ch

    def flip(src, dst):
        for tap in range(27):
            dst[tap * ch : (tap + 1) * ch, :] = src[tap * ch : (tap + 1) * ch, :].T

    if part > quarter:
        early_out[...] = jnp.zeros(early_out.shape, BF16)
        late_out[...] = jnp.zeros(late_out.shape, BF16)
    lane = lax.broadcasted_iota(jnp.int32, (16, 2 * slab), 1)
    frame = lax.rem(lax.div(lane, cols), frames)
    number = jnp.zeros((16, 2 * slab), F32)
    for f in range(frames):
        number = jnp.where(frame == f, seg[0, f].astype(F32), number)
    for q in range(n_dp):
        early_out[q, seg_at : seg_at + 16, :] = number.astype(BF16)

    @pl.when(tile == 0)
    def _():
        x_halo[0] = jnp.zeros(x_halo.shape[1:], BF16)
        g_halo[0] = jnp.zeros(g_halo.shape[1:], BF16)

    @pl.when(tile == n_tile - 1)
    def _():
        x_halo[1] = jnp.zeros(x_halo.shape[1:], BF16)
        g_halo[1] = jnp.zeros(g_halo.shape[1:], BF16)

    for copy in load_x + load_c:
        copy.wait()
    beside = jnp.where(tile > 0, 1, 0) + jnp.where(tile < n_tile - 1, 1, 0)
    pl.semaphore_wait(barrier, n_dp - 1 + n_z - 1 + beside)

    g_rows = c_in.shape[0]
    c_flat[...] = c_in[...].astype(F32).reshape(cells // 4, ch).astype(BF16)

    def halo(side):
        peer = {"tile": tile - 1 if side == 0 else tile + 1}
        return (
            pltpu.make_async_remote_copy(
                src_ref=x_in.at[0:2] if side == 0 else x_in.at[rows - 2 : rows],
                dst_ref=x_halo.at[1 - side],
                send_sem=h_send.at[side], recv_sem=h_recv.at[1 - side],
                device_id=peer, device_id_type=MESH,
            ),
            pltpu.make_async_remote_copy(
                src_ref=c_flat.at[0 : slab // 2]
                if side == 0
                else c_flat.at[(g_rows - 1) * slab // 2 : g_rows * slab // 2],
                dst_ref=g_halo.at[1 - side],
                send_sem=h_send.at[2 + side], recv_sem=h_recv.at[2 + 1 - side],
                device_id=peer, device_id_type=MESH,
            ),
        )

    @pl.when(tile > 0)
    def _():
        for copy in halo(0):
            copy.start()

    @pl.when(tile < n_tile - 1)
    def _():
        for copy in halo(1):
            copy.start()

    def to_dp(src, dst, sends, recvs):
        return [
            pltpu.make_async_remote_copy(
                src_ref=src(lax.rem(dp + i, n_dp)), dst_ref=dst,
                send_sem=sends.at[i - 1], recv_sem=recvs.at[i - 1],
                device_id={"dp": lax.rem(dp + i, n_dp)}, device_id_type=MESH,
            )
            for i in range(1, n_dp)
        ]

    def start(copies):
        for copy in copies:
            copy.start()

    def wait(copies):
        for copy in copies:
            copy.wait()

    def deal(v, out, base):
        v = v.reshape(-1, ch).T.astype(BF16)
        for p in range(v.shape[1] // ch):
            for q in range(n_dp):
                at = base + p * part
                out[q, at : at + quarter, :] = v[q * quarter : (q + 1) * quarter, p * ch : (p + 1) * ch]

    def dealt(got, d, base, n):
        return [got[d, base + p * part : base + (p + 1) * part, :].astype(F32) for p in range(n)]

    mine = x_in[...].astype(F32)
    for q in range(n_dp):
        early_out[q, cot_at:seg_at, :] = c_flat[...]
    deal(mine, early_out, 0)
    copies_early = to_dp(lambda q: early_out.at[q], early_got.at[dp], x_send, x_recv)
    start(copies_early)
    early_got[dp] = early_out[dp]

    load_w2.wait()
    flip(w2, w2t)
    same = [None]
    for t in range(1, 3):
        same.append(
            [None] * t
            + [jnp.where(seg[0, f] == seg[0, f - t], 1.0, 0.0).astype(F32) for f in range(t, frames)]
        )

    def four(v):
        return v.reshape(v.shape[0], frames, cols, ch)

    def grow(v):
        n = v.shape[0] * 2 // slab
        v = v.astype(F32) * 0.25
        g_tmp[pl.ds(0, n * slab // 2, stride=2), :] = v
        g_tmp[pl.ds(1, n * slab // 2, stride=2), :] = v
        v = g_tmp[0 : n * slab, :].reshape(n, slab, ch)
        return jnp.stack([v, v], axis=1).reshape(2 * n, slab, ch)

    g_mine = grow(c_flat[...])
    fill_columns(cols_g, four(g_mine), same, True, 2)
    own_g[...] = own_dots(cols_g, w2t, rows, slab, True)
    fill_columns(cols_x, mine, same, False, 2)
    load_w1.wait()
    own_x[...] = own_dots(cols_x, w1, rows, slab, False)

    @pl.when(tile > 0)
    def _():
        for copy in halo(0):
            copy.wait_send()
        for copy in halo(1):
            copy.wait_recv()

    @pl.when(tile < n_tile - 1)
    def _():
        for copy in halo(1):
            copy.wait_send()
        for copy in halo(0):
            copy.wait_recv()

    x_low = x_halo[0].astype(F32)
    x_high = x_halo[1].astype(F32)
    deal(jnp.concatenate([x_high[:1], x_low[1:]], axis=0), late_out, edge_at)
    fill_columns(cols_x, x_low, same, False, 0)
    fill_columns(cols_x, x_high, same, False, rows + 2)
    first = own_x[...] + edge_dots(cols_x, w1, rows, slab, False)
    sigma = 1.0 / (1.0 + jnp.exp(-first))
    copies_hid = to_dp(lambda q: late_out.at[q], late_got.at[dp], t_send, t_recv)
    copies_act = to_dp(lambda q: act_got.at[dp], act_got.at[dp], g_send, g_recv)

    top = jnp.where(tile > 0, 1.0, 0.0).astype(F32)
    low = jnp.where(tile < n_tile - 1, 1.0, 0.0).astype(F32)

    def edges(v):
        v = v.reshape(wide, slab, ch)
        return jnp.concatenate([v[:1] * top, v[1:-1], v[-1:] * low], axis=0)

    def first_unit(to, q):
        unit_at = lax.div(share, unit) * to
        beyond = jnp.clip(lax.rem(unit_at, per_tap) - per_quarter * q, 0, per_quarter)
        return jnp.minimum(per_quarter * lax.div(unit_at, per_tap) + beyond, taps * per_quarter - n_unit)

    def window(to):
        return pl.ds(pl.multiple_of(first_unit(to, dp) * slot, 16), block)

    def copies_a(g):
        return [
            pltpu.make_async_remote_copy(
                src_ref=flat.at[g, window(2 * lax.rem(z + j, n_z) + 1 - core)], dst_ref=recv_a.at[g, j],
                send_sem=a_send.at[g, j], recv_sem=a_recv.at[g, j],
                device_id={"tile": tile + 1 - 2 * core}, device_id_type=MESH,
            )
            for j in range(n_z)
        ]

    def copies_c(g):
        return [
            pltpu.make_async_remote_copy(
                src_ref=send_c.at[g, j - 1], dst_ref=recv_c.at[g, j - 1],
                send_sem=c_send.at[g, j - 1], recv_sem=c_recv.at[g, j - 1],
                device_id={"tile": 2 * lax.rem(z + j, n_z) + core}, device_id_type=MESH,
            )
            for j in range(1, n_z)
        ]

    def copies_d(g):
        return to_dp(lambda q: every.at[g, dp], every.at[g, dp], d_send.at[g], d_recv.at[g])

    def sender(i):
        return lax.rem(dp + n_dp - i, n_dp)

    def make_masks(d):
        number = early_got[d, seg_at : seg_at + 16, :].astype(F32)[0:8]
        at = lax.broadcasted_iota(jnp.int32, (8, 2 * slab), 1)
        when = lax.rem(lax.div(at, cols), frames)
        col = lax.rem(at, cols)
        for t in range(3):
            keep = jnp.ones((8, 2 * slab), F32)
            if t > 0:
                keep = jnp.where(number == pltpu.roll(number, t * cols, 1), 1.0, 0.0)
                keep = jnp.where(when >= t, keep, 0.0)
            for b in range(3):
                inside = jnp.where((col + (b - 1) >= 0) & (col + (b - 1) < cols), keep, 0.0)
                mask_rows[d, t * 3 + b] = inside

    def turn(g, d, v):
        for t in range(3):
            for b in range(3):
                shift = t * cols - (b - 1)
                moved = v if shift == 0 else pltpu.roll(v, shift % lanes, 1)
                if t > 0 or b != 1:
                    keep = jnp.concatenate([mask_rows[d, t * 3 + b]] * (wide // 2), axis=1)
                    moved = moved * jnp.concatenate([keep] * (part // 8), axis=0)
                for a in range(3):
                    w = moved if a == 1 else pltpu.roll(moved, (1 - a) * slab % lanes, 1)
                    at = ((t * 3 + a) * 3 + b) * part
                    turned[g, d, at : at + part, :] = w[:, 0:cells].astype(BF16)

    def partial_sum(g, d, right, fresh):
        term = jnp.dot(turned[g, d], right, preferred_element_type=F32)
        flat[g] = term if fresh else flat[g] + term

    def step_a(g):
        copies = copies_a(g)
        for j in (*range(1, n_z), 0):
            copies[j].start()

    def step_b(g):
        pairs, sends = copies_a(g), copies_c(g)
        for j in (*range(1, n_z), 0):
            pairs[j].wait()
            total = flat[g, window(2 * lax.rem(z + j, n_z) + core), :] + recv_a[g, j]
            if j > 0:
                send_c[g, j - 1] = total.astype(BF16)
                sends[j - 1].start()
            else:
                sum_a[g] = total

    def step_c(g):
        wait(copies_c(g))
        total = sum_a[g]
        for j in range(1, n_z):
            total = total + recv_c[g, j - 1].astype(F32)
        every[g, dp] = (total * scale).astype(BF16)
        start(copies_d(g))

    def step_d(g):
        wait(copies_d(g))
        for q in range(n_dp):
            v = every[g, q].astype(F32)
            for i in range(n_unit):
                u = first_unit(tile, q) + i
                at = ch * lax.div(u, per_quarter) + unit * lax.rem(u, per_quarter) + quarter * q - share * tile
                at = pl.multiple_of(at + margin, 8)
                spread[g, pl.ds(at, unit), :] = v[i * slot : i * slot + unit]
        outs[g][...] = spread[g, margin : margin + share, :]

    hidden = edges(first * sigma)
    by_row = hidden.reshape(wide, slab, ch)
    deal(jnp.concatenate([by_row[1:], by_row[:1]], axis=0), late_out, 0)
    start(copies_hid)
    late_got[dp] = late_out[dp]
    g_own = g_mine.reshape(cells, ch)
    fill_columns(cols_g, four(grow(g_halo[0])), same, True, 0)
    fill_columns(cols_g, four(grow(g_halo[1])), same, True, rows + 2)
    hidden_grad = own_g[...] + edge_dots(cols_g, w2t, rows, slab, True)
    act = edges(hidden_grad * sigma * (1.0 + first * (1.0 - sigma)))
    act_got[dp] = act[1 : 1 + rows].reshape(cells, ch).astype(BF16)
    start(copies_act)
    flip(w1, w1t)

    wait(copies_early)
    for d in range(n_dp):
        make_masks(d)
        g_got[d] = grow(early_got[d, cot_at:seg_at, :]).reshape(cells, ch).astype(BF16)
    fill_columns(cols_h, four(hidden), same, False)
    for i in range(n_dp):
        if i > 0:
            copies_hid[i - 1].wait()
        parts = dealt(late_got, sender(i), 0, own_lanes + 1)
        turn(1, sender(i), jnp.concatenate(parts, axis=1))
        partial_sum(1, sender(i), g_got[sender(i)], i == 0)
    step_a(1)
    for d in range(n_dp):
        parts = dealt(early_got, d, 0, own_lanes) + dealt(late_got, d, edge_at, 1)
        turn(0, d, jnp.concatenate(parts, axis=1))
    step_b(1)
    for i in range(n_dp):
        if i > 0:
            copies_act[i - 1].wait()
        partial_sum(0, sender(i), act_got[sender(i)], i == 0)
    step_a(0)
    step_b(0)

    second = conv_dots(cols_h, w2, 0, rows, slab, False)
    summed = mine.reshape(rows, slab, ch) + second.reshape(rows, slab, ch)
    pairs = rows // 2
    for i in range(pairs):
        pool_tmp[i * slab : (i + 1) * slab, :] = summed[2 * i] + summed[2 * i + 1]
    for i in range(pairs):
        for f in range(frames):
            at = i * slab + f * cols
            pooled[0, f, i] = 0.25 * (
                pool_tmp[pl.ds(at, cols // 2, stride=2), :]
                + pool_tmp[pl.ds(at + 1, cols // 2, stride=2), :]
            )
    fill_columns(cols_a, four(act), same, True)
    back = conv_dots(cols_a, w1t, 0, rows, slab, True)
    total = (g_own + back).reshape(rows, frames, cols, ch)
    for r in range(rows):
        in_grad[0, :, r] = total[r]
    step_c(1)
    step_c(0)
    step_d(1)
    step_d(0)


def hand_out(*refs):
    sems = refs[8]
    copies = [pltpu.make_async_copy(refs[i], refs[4 + i], sems.at[i]) for i in (1, 2, 3, 0)]
    for copy in copies:
        copy.start()
    for copy in copies:
        copy.wait()


def local(n_tile, n_dp, clip_frames, segments, weight_first, weight_second, cotangent):
    _, frames, rows, cols, ch = clip_frames.shape
    slab = frames * cols
    taps = weight_first.shape[0]
    share = taps // n_tile
    n_z = n_tile // 2
    quarter = ch // n_dp
    part = up16(quarter)
    unit = math.gcd(share, quarter)
    per_quarter = quarter // unit

    def before(to, q):
        whole, rest = divmod(share // unit * to, ch // unit)
        return per_quarter * whole + min(max(rest - per_quarter * q, 0), per_quarter)

    n_unit = max(before(k + 1, q) - before(k, q) for k in range(n_tile) for q in range(n_dp))
    block = n_unit * (part // per_quarter)
    span = share + 2 * ch * (n_unit // per_quarter + 2)
    scale = 1.0 / math.sqrt(n_dp * n_tile * rows * slab)
    vmem = pl.BlockSpec(memory_space=pltpu.VMEM)
    cells = rows * slab
    lanes = (rows + 2) * slab
    sem = pltpu.SemaphoreType.DMA
    anywhere = pl.BlockSpec(memory_space=pltpu.HBM)
    shapes = (
        jax.ShapeDtypeStruct((1, frames, rows // 2, cols // 2, ch), F32),
        jax.ShapeDtypeStruct((1, frames, rows, cols, ch), F32),
        jax.ShapeDtypeStruct((share, ch), F32),
        jax.ShapeDtypeStruct((share, ch), F32),
    )
    held = [
        pltpu.with_memory_space_constraint(v, pltpu.HBM)
        for v in (segments, clip_frames, weight_first, weight_second, cotangent)
    ]
    results = pl.pallas_call(
        functools.partial(kernel, (n_tile, n_dp, share, quarter, part, unit, n_unit, scale)),
        out_shape=shapes,
        in_specs=[pl.BlockSpec(memory_space=pltpu.SMEM)] + [anywhere] * 4,
        out_specs=(vmem,) * 4,
        scratch_shapes=[
            pltpu.VMEM((rows, frames, cols, ch), BF16),
            pltpu.VMEM((taps, ch), BF16),
            pltpu.VMEM((taps, ch), BF16),
            pltpu.VMEM((rows // 2, frames, cols // 2, ch), BF16),
            pltpu.VMEM(((rows // 2 + 2) * slab, ch), F32),
            sem((2 + rows + rows // 2,)),
            pltpu.VMEM((2, 2, frames, cols, ch), BF16),
            pltpu.VMEM((2, frames * cols // 2, ch), BF16),
            pltpu.VMEM(((rows + 4) * slab, 9 * ch), BF16),
            pltpu.VMEM(((rows + 2) * slab, 9 * ch), BF16),
            pltpu.VMEM(((rows + 4) * slab, 9 * ch), BF16),
            pltpu.VMEM(((rows + 2) * slab, 9 * ch), BF16),
            pltpu.VMEM((taps, ch), BF16),
            pltpu.VMEM((taps, ch), BF16),
            pltpu.VMEM((cells // 2, ch), F32),
            pltpu.VMEM((lanes, ch), F32),
            pltpu.VMEM((lanes, ch), F32),
            pltpu.VMEM((n_dp, 9, 8, 2 * slab), F32),
            pltpu.VMEM((cells // 4, ch), BF16),
            pltpu.VMEM((n_dp, cells // ch * part + cells // 4 + 16, ch), BF16),
            pltpu.VMEM((n_dp, cells // ch * part + cells // 4 + 16, ch), BF16),
            pltpu.VMEM((n_dp, (cells // ch + 2) * part, ch), BF16),
            pltpu.VMEM((n_dp, (cells // ch + 2) * part, ch), BF16),
            pltpu.VMEM((n_dp, cells, ch), BF16),
            pltpu.VMEM((n_dp, cells, ch), BF16),
            pltpu.VMEM((2, n_dp, taps // ch * part, cells), BF16),
            pltpu.VMEM((2, taps // ch * part, ch), F32),
            pltpu.VMEM((2, n_z, block, ch), F32),
            pltpu.VMEM((2, block, ch), F32),
            pltpu.VMEM((2, n_z - 1, block, ch), BF16),
            pltpu.VMEM((2, n_z - 1, block, ch), BF16),
            pltpu.VMEM((2, n_dp, block, ch), BF16),
            pltpu.VMEM((2, span, ch), F32),
            sem((4,)), sem((4,)),
            sem((n_dp - 1,)), sem((n_dp - 1,)),
            sem((n_dp - 1,)), sem((n_dp - 1,)),
            sem((n_dp - 1,)), sem((n_dp - 1,)),
            sem((2, n_z)), sem((2, n_z)),
            sem((2, n_z - 1)), sem((2, n_z - 1)),
            sem((2, n_dp - 1)), sem((2, n_dp - 1)),
        ],
        compiler_params=pltpu.CompilerParams(
            collective_id=0, has_side_effects=True, vmem_limit_bytes=50 * 1024 * 1024
        ),
    )(*held)
    return tuple(
        pl.pallas_call(
            hand_out,
            out_shape=shapes,
            in_specs=[pl.BlockSpec(memory_space=pl.ANY)] * 4,
            out_specs=(pl.BlockSpec(memory_space=pl.ANY),) * 4,
            scratch_shapes=[sem((4,))],
            compiler_params=pltpu.CompilerParams(vmem_limit_bytes=4 * 1024 * 1024),
        )(*results)
    )


def solution(mesh):
    return jax.shard_map(
        functools.partial(local, mesh.shape["tile"], mesh.shape["dp"]),
        mesh=mesh,
        in_specs=(
            P("dp", None, "tile", None, None),
            P("dp", None),
            P(),
            P(),
            P("dp", None, "tile", None, None),
        ),
        out_specs=(
            P("dp", None, "tile", None, None),
            P("dp", None, "tile", None, None),
            P("tile", None),
            P("tile", None),
        ),
        check_vma=False,
    )
```

```python
import functools
import math

import jax
import jax.numpy as jnp
from jax import lax
from jax.experimental import pallas as pl
from jax.experimental.pallas import tpu as pltpu
from jax.sharding import PartitionSpec as P

MESH = pl.DeviceIdType.MESH
F32 = jnp.float32
BF16 = jnp.bfloat16


def up16(n):
    return -(-n // 16) * 16


def shifted_cols(cells, step):
    if step == 0:
        return cells
    cols = cells.shape[2]
    col = lax.broadcasted_iota(jnp.int32, cells.shape, 2)
    moved = pltpu.roll(cells, (-step) % cols, 2)
    keep = (col < cols - 1) if step == 1 else (col > 0)
    return jnp.where(keep, moved, 0.0)


def fill_columns(dst, cells, same, reverse, first=0):
    rows, frames, cols, ch = cells.shape
    for ci in range(3):
        moved = shifted_cols(cells, (1 - ci) if reverse else (ci - 1))
        for t in range(3):
            zero = jnp.zeros((rows, cols, ch), F32)
            parts = []
            for f in range(frames):
                src = f + t if reverse else f - t
                if src < 0 or src >= frames:
                    parts.append(zero)
                elif t == 0:
                    parts.append(moved[:, src])
                else:
                    parts.append(moved[:, src] * same[t][max(f, src)])
            block = jnp.stack(parts, axis=1).reshape(rows * frames * cols, ch)
            at = (t * 3 + ci) * ch
            from_row = first * frames * cols
            dst[from_row : from_row + rows * frames * cols, at : at + ch] = block.astype(BF16)


def conv_dots(cols_ref, w_ref, start, rows, slab, reverse):
    acc = None
    span = w_ref.shape[1] * 3
    for t in range(3):
        for a in range(3):
            at = (start + (2 - a if reverse else a)) * slab
            term = jnp.dot(
                cols_ref[at : at + rows * slab, t * span : (t + 1) * span],
                w_ref[(t * 3 + a) * span : (t * 3 + a + 1) * span, :],
                preferred_element_type=F32,
            )
            acc = term if acc is None else acc + term
    return acc


def own_dots(cols_ref, w_ref, rows, slab, reverse):
    total = None
    span = w_ref.shape[1] * 3
    for a in range(3):
        e = 2 - a if reverse else a
        term = None
        for t in range(3):
            one = jnp.dot(
                cols_ref[2 * slab : (2 + rows) * slab, t * span : (t + 1) * span],
                w_ref[(t * 3 + a) * span : (t * 3 + a + 1) * span, :],
                preferred_element_type=F32,
            )
            term = one if term is None else term + one
        ends = [jnp.zeros((n * slab, w_ref.shape[1]), F32) for n in (2 - e, e)]
        parts = [v for v in (ends[0], term, ends[1]) if v.shape[0] > 0]
        padded = jnp.concatenate(parts, axis=0)
        total = padded if total is None else total + padded
    return total


def edge_dots(cols_ref, w_ref, rows, slab, reverse):
    terms = []
    span = w_ref.shape[1] * 3
    for e in range(3):
        a = 2 - e if reverse else e
        term = None
        for t in range(3):
            at = slice(t * span, (t + 1) * span)
            if e == 0:
                left = cols_ref[0 : 2 * slab, at]
            elif e == 1:
                left = jnp.concatenate(
                    [cols_ref[slab : 2 * slab, at], cols_ref[(rows + 2) * slab : (rows + 3) * slab, at]], axis=0
                )
            else:
                left = cols_ref[(rows + 2) * slab : (rows + 4) * slab, at]
            one = jnp.dot(
                left, w_ref[(t * 3 + a) * span : (t * 3 + a + 1) * span, :], preferred_element_type=F32
            )
            term = one if term is None else term + one
        terms.append(term)
    return jnp.concatenate(
        [
            terms[0][:slab] + terms[1][:slab],
            terms[0][slab:],
            jnp.zeros(((rows - 2) * slab, w_ref.shape[1]), F32),
            terms[2][:slab],
            terms[2][slab:] + terms[1][slab:],
        ],
        axis=0,
    )


def kernel(
    cfg,
    seg, x_hbm, w1_hbm, w2_hbm, c_hbm,
    pooled, in_grad, out1, out2,
    x_in, w1, w2, c_in, g_tmp, in_sem, edge_out, edge_in, cols_x, cols_h, cols_g, cols_a, w1t, w2t, pool_tmp,
    own_x, own_g, mid_got, mask_rows, c_flat, early_out, early_got, late_out, late_got, act_got, g_got, turned, flat,
    recv_a, sum_a, send_c, recv_c, every, spread,
    h_send, h_recv, m_send, m_recv, x_send, x_recv, g_send, g_recv, t_send, t_recv,
    a_send, a_recv, c_send, c_recv, d_send, d_recv,
):
    n_tile, n_dp, share, quarter, part, unit, n_unit, scale = cfg
    n_z = n_tile // 2
    rows, frames, cols, ch = x_in.shape
    slab = frames * cols
    tile = lax.axis_index("tile")
    dp = lax.axis_index("dp")
    core = lax.rem(tile, 2)
    z = lax.div(tile, 2)
    taps = w1.shape[0] // ch
    outs = (out1, out2)
    wide = rows + 2
    cells = rows * slab
    lanes = wide * slab
    per_tap, per_quarter = ch // unit, quarter // unit
    slot = part // per_quarter
    own_lanes = cells // ch
    cot_at = own_lanes * part
    seg_at = cot_at + cells // 4
    edge_at = (own_lanes + 1) * part
    margin = (spread.shape[1] - share) // 2
    block = n_unit * slot

    load_x = [
        pltpu.make_async_copy(x_hbm.at[0, :, r], x_in.at[r], in_sem.at[2 + r]) for r in range(rows)
    ]
    load_c = [
        pltpu.make_async_copy(c_hbm.at[0, :, r], c_in.at[r], in_sem.at[2 + rows + r])
        for r in range(rows // 2)
    ]
    load_w1 = pltpu.make_async_copy(w1_hbm, w1, in_sem.at[0])
    load_w2 = pltpu.make_async_copy(w2_hbm, w2, in_sem.at[1])
    for copy in load_x + load_c:
        copy.start()
    load_w1.start()
    load_w2.start()

    barrier = pltpu.get_barrier_semaphore()

    def greet(peer):
        pl.semaphore_signal(barrier, inc=1, device_id=peer, device_id_type=MESH)

    @pl.when(tile > 0)
    def _():
        greet({"tile": tile - 1})

    @pl.when(tile < n_tile - 1)
    def _():
        greet({"tile": tile + 1})

    for i in range(1, n_dp):
        greet({"dp": lax.rem(dp + i, n_dp)})
    for j in range(1, n_z):
        greet({"tile": 2 * lax.rem(z + j, n_z) + core})

    span = 3 * ch

    def flip(src, dst):
        for tap in range(27):
            dst[tap * ch : (tap + 1) * ch, :] = src[tap * ch : (tap + 1) * ch, :].T

    if part > quarter:
        early_out[...] = jnp.zeros(early_out.shape, BF16)
        late_out[...] = jnp.zeros(late_out.shape, BF16)
    lane = lax.broadcasted_iota(jnp.int32, (16, 2 * slab), 1)
    frame = lax.rem(lax.div(lane, cols), frames)
    number = jnp.zeros((16, 2 * slab), F32)
    for f in range(frames):
        number = jnp.where(frame == f, seg[0, f].astype(F32), number)
    for q in range(n_dp):
        early_out[q, seg_at : seg_at + 16, :] = number.astype(BF16)

    @pl.when(tile == 0)
    def _():
        edge_in[0] = jnp.zeros(edge_in.shape[1:], BF16)

    @pl.when(tile == n_tile - 1)
    def _():
        edge_in[1] = jnp.zeros(edge_in.shape[1:], BF16)

    for copy in load_x + load_c:
        copy.wait()
    c_flat[...] = c_in[...].astype(F32).reshape(cells // 4, ch).astype(BF16)
    mine = x_in[...].astype(F32)
    flat_x = mine.reshape(cells, ch).astype(BF16)
    edge_out[0, 0 : 2 * slab, :] = flat_x[: 2 * slab]
    edge_out[1, 0 : 2 * slab, :] = flat_x[cells - 2 * slab :]
    edge_out[0, 2 * slab :, :] = c_flat[0 : slab // 2, :]
    edge_out[1, 2 * slab :, :] = c_flat[cells // 4 - slab // 2 :, :]
    def deal(v, out, base):
        v = v.reshape(-1, ch).T.astype(BF16)
        for p in range(v.shape[1] // ch):
            for q in range(n_dp):
                at = base + p * part
                out[q, at : at + quarter, :] = v[q * quarter : (q + 1) * quarter, p * ch : (p + 1) * ch]

    for q in range(n_dp):
        early_out[q, cot_at:seg_at, :] = c_flat[...]
    deal(mine, early_out, 0)
    same = [None]
    for t in range(1, 3):
        same.append(
            [None] * t
            + [jnp.where(seg[0, f] == seg[0, f - t], 1.0, 0.0).astype(F32) for f in range(t, frames)]
        )

    def four(v):
        return v.reshape(v.shape[0], frames, cols, ch)

    def grow(v):
        n = v.shape[0] * 2 // slab
        v = v.astype(F32) * 0.25
        g_tmp[pl.ds(0, n * slab // 2, stride=2), :] = v
        g_tmp[pl.ds(1, n * slab // 2, stride=2), :] = v
        v = g_tmp[0 : n * slab, :].reshape(n, slab, ch)
        return jnp.stack([v, v], axis=1).reshape(2 * n, slab, ch)

    g_mine = grow(c_flat[...])
    fill_columns(cols_g, four(g_mine), same, True, 2)
    fill_columns(cols_x, mine, same, False, 2)
    beside = jnp.where(tile > 0, 1, 0) + jnp.where(tile < n_tile - 1, 1, 0)
    pl.semaphore_wait(barrier, n_dp - 1 + n_z - 1 + beside)


    def halo(side):
        return [
            pltpu.make_async_remote_copy(
                src_ref=edge_out.at[side], dst_ref=edge_in.at[1 - side],
                send_sem=h_send.at[side], recv_sem=h_recv.at[1 - side],
                device_id={"tile": tile - 1 if side == 0 else tile + 1}, device_id_type=MESH,
            )
        ]

    @pl.when(tile > 0)
    def _():
        for copy in halo(0):
            copy.start()

    @pl.when(tile < n_tile - 1)
    def _():
        for copy in halo(1):
            copy.start()

    def to_dp(src, dst, sends, recvs):
        return [
            pltpu.make_async_remote_copy(
                src_ref=src(lax.rem(dp + i, n_dp)), dst_ref=dst,
                send_sem=sends.at[i - 1], recv_sem=recvs.at[i - 1],
                device_id={"dp": lax.rem(dp + i, n_dp)}, device_id_type=MESH,
            )
            for i in range(1, n_dp)
        ]

    def start(copies):
        for copy in copies:
            copy.start()

    def wait(copies):
        for copy in copies:
            copy.wait()

    def dealt(got, d, base, n):
        return [got[d, base + p * part : base + (p + 1) * part, :].astype(F32) for p in range(n)]

    copies_early = to_dp(lambda q: early_out.at[q], early_got.at[dp], x_send, x_recv)
    start(copies_early)
    early_got[dp] = early_out[dp]

    load_w2.wait()
    flip(w2, w2t)
    own_g[...] = own_dots(cols_g, w2t, rows, slab, True)
    load_w1.wait()
    own_x[...] = own_dots(cols_x, w1, rows, slab, False)
    middle = slice(2 * slab, rows * slab)
    inner = (rows - 2) * slab
    mid = own_x[middle, :]
    mid_sigma = 1.0 / (1.0 + jnp.exp(-mid))
    mid_act = own_g[middle, :] * mid_sigma * (1.0 + mid * (1.0 - mid_sigma))
    mid_got[dp] = mid_act.astype(BF16)
    copies_mid = to_dp(lambda q: mid_got.at[dp], mid_got.at[dp], m_send, m_recv)
    start(copies_mid)

    @pl.when(tile > 0)
    def _():
        for copy in halo(0):
            copy.wait_send()
        for copy in halo(1):
            copy.wait_recv()

    @pl.when(tile < n_tile - 1)
    def _():
        for copy in halo(1):
            copy.wait_send()
        for copy in halo(0):
            copy.wait_recv()

    x_low, x_high = (edge_in[n, 0 : 2 * slab, :].astype(F32).reshape(2, frames, cols, ch) for n in range(2))
    deal(jnp.concatenate([x_high[:1], x_low[1:]], axis=0), late_out, edge_at)
    fill_columns(cols_x, x_low, same, False, 0)
    fill_columns(cols_x, x_high, same, False, rows + 2)
    first = own_x[...] + edge_dots(cols_x, w1, rows, slab, False)
    sigma = 1.0 / (1.0 + jnp.exp(-first))
    copies_hid = to_dp(lambda q: late_out.at[q], late_got.at[dp], t_send, t_recv)
    copies_act = to_dp(lambda q: act_got.at[dp], act_got.at[dp], g_send, g_recv)

    top = jnp.where(tile > 0, 1.0, 0.0).astype(F32)
    low = jnp.where(tile < n_tile - 1, 1.0, 0.0).astype(F32)

    def edges(v):
        v = v.reshape(wide, slab, ch)
        return jnp.concatenate([v[:1] * top, v[1:-1], v[-1:] * low], axis=0)

    def first_unit(to, q):
        unit_at = lax.div(share, unit) * to
        beyond = jnp.clip(lax.rem(unit_at, per_tap) - per_quarter * q, 0, per_quarter)
        return jnp.minimum(per_quarter * lax.div(unit_at, per_tap) + beyond, taps * per_quarter - n_unit)

    def window(to):
        return pl.ds(pl.multiple_of(first_unit(to, dp) * slot, 16), block)

    def copies_a(g):
        return [
            pltpu.make_async_remote_copy(
                src_ref=flat.at[g, window(2 * lax.rem(z + j, n_z) + 1 - core)], dst_ref=recv_a.at[g, j],
                send_sem=a_send.at[g, j], recv_sem=a_recv.at[g, j],
                device_id={"tile": tile + 1 - 2 * core}, device_id_type=MESH,
            )
            for j in range(n_z)
        ]

    def copies_c(g):
        return [
            pltpu.make_async_remote_copy(
                src_ref=send_c.at[g, j - 1], dst_ref=recv_c.at[g, j - 1],
                send_sem=c_send.at[g, j - 1], recv_sem=c_recv.at[g, j - 1],
                device_id={"tile": 2 * lax.rem(z + j, n_z) + core}, device_id_type=MESH,
            )
            for j in range(1, n_z)
        ]

    def copies_d(g):
        return to_dp(lambda q: every.at[g, dp], every.at[g, dp], d_send.at[g], d_recv.at[g])

    def sender(i):
        return lax.rem(dp + n_dp - i, n_dp)

    def make_masks(d):
        number = early_got[d, seg_at : seg_at + 16, :].astype(F32)[0:8]
        at = lax.broadcasted_iota(jnp.int32, (8, 2 * slab), 1)
        when = lax.rem(lax.div(at, cols), frames)
        col = lax.rem(at, cols)
        for t in range(3):
            keep = jnp.ones((8, 2 * slab), F32)
            if t > 0:
                keep = jnp.where(number == pltpu.roll(number, t * cols, 1), 1.0, 0.0)
                keep = jnp.where(when >= t, keep, 0.0)
            for b in range(3):
                inside = jnp.where((col + (b - 1) >= 0) & (col + (b - 1) < cols), keep, 0.0)
                mask_rows[d, t * 3 + b] = inside

    def put(g, d, piece, uses):
        for t in range(3):
            for b in range(3):
                shift = t * cols - (b - 1)
                moved = piece if shift == 0 else pltpu.roll(piece, shift % (2 * slab), 1)
                if t > 0 or b != 1:
                    keep = mask_rows[d, t * 3 + b]
                    moved = moved * jnp.concatenate([keep] * (part // 8), axis=0)
                moved = moved.astype(BF16)
                for a, k in uses:
                    at = ((t * 3 + a) * 3 + b) * part
                    turned[g, d, at : at + part, k * ch : (k + 1) * ch] = moved

    def between(before, after):
        lower = lax.broadcasted_iota(jnp.int32, before.shape, 1) < slab
        return jnp.where(lower, pltpu.roll(before, slab, 1), pltpu.roll(after, slab, 1))

    def turn_own(g, d, own):
        for k, piece in enumerate(own):
            put(g, d, piece, [(1, k)])
            if k > 0:
                put(g, d, between(own[k - 1], piece), [(0, k), (2, k - 1)])

    def turn_ends(g, d, own, ends):
        put(g, d, between(ends, own[0]), [(0, 0)])
        put(g, d, between(own[-1], ends), [(2, len(own) - 1)])

    def partial_sum(g, d, right, fresh):
        term = jnp.dot(turned[g, d], right, preferred_element_type=F32)
        flat[g] = term if fresh else flat[g] + term

    def step_a(g):
        copies = copies_a(g)
        for j in (*range(1, n_z), 0):
            copies[j].start()

    def step_b(g):
        pairs, sends = copies_a(g), copies_c(g)
        for j in (*range(1, n_z), 0):
            pairs[j].wait()
            total = flat[g, window(2 * lax.rem(z + j, n_z) + core), :] + recv_a[g, j]
            if j > 0:
                send_c[g, j - 1] = total.astype(BF16)
                sends[j - 1].start()
            else:
                sum_a[g] = total

    def step_c(g):
        wait(copies_c(g))
        total = sum_a[g]
        for j in range(1, n_z):
            total = total + recv_c[g, j - 1].astype(F32)
        every[g, dp] = (total * scale).astype(BF16)
        start(copies_d(g))

    def step_d(g):
        wait(copies_d(g))
        for q in range(n_dp):
            v = every[g, q].astype(F32)
            for i in range(n_unit):
                u = first_unit(tile, q) + i
                at = ch * lax.div(u, per_quarter) + unit * lax.rem(u, per_quarter) + quarter * q - share * tile
                at = pl.multiple_of(at + margin, 8)
                spread[g, pl.ds(at, unit), :] = v[i * slot : i * slot + unit]
        outs[g][...] = spread[g, margin : margin + share, :]

    hidden = edges(first * sigma)
    by_row = hidden.reshape(wide, slab, ch)
    deal(jnp.concatenate([by_row[1:], by_row[:1]], axis=0), late_out, 0)
    start(copies_hid)
    late_got[dp] = late_out[dp]
    g_own = g_mine.reshape(cells, ch)
    fill_columns(cols_g, four(grow(edge_in[0, 2 * slab :, :])), same, True, 0)
    fill_columns(cols_g, four(grow(edge_in[1, 2 * slab :, :])), same, True, rows + 2)
    hidden_grad = own_g[...] + edge_dots(cols_g, w2t, rows, slab, True)
    act = edges(hidden_grad * sigma * (1.0 + first * (1.0 - sigma)))
    act_got[dp] = jnp.concatenate([act[1], act[rows]], axis=0).astype(BF16)
    start(copies_act)
    flip(w1, w1t)

    wait(copies_early)
    for d in range(n_dp):
        make_masks(d)
        g_got[d] = grow(early_got[d, cot_at:seg_at, :]).reshape(cells, ch).astype(BF16)
        turn_own(0, d, dealt(early_got, d, 0, own_lanes))
    fill_columns(cols_h, four(hidden), same, False)
    for i in range(n_dp):
        if i > 0:
            copies_hid[i - 1].wait()
        *own, ends = dealt(late_got, sender(i), 0, own_lanes + 1)
        turn_own(1, sender(i), own)
        turn_ends(1, sender(i), own, ends)
        partial_sum(1, sender(i), g_got[sender(i)], i == 0)
    step_a(1)
    for d in range(n_dp):
        turn_ends(0, d, dealt(early_got, d, 0, own_lanes), dealt(late_got, d, edge_at, 1)[0])
    step_b(1)
    for i in range(n_dp):
        d = sender(i)
        if i > 0:
            copies_mid[i - 1].wait()
            copies_act[i - 1].wait()
        ends = act_got[d]
        partial_sum(0, d, jnp.concatenate([ends[:slab], mid_got[d], ends[slab:]], axis=0), i == 0)
    step_a(0)
    step_b(0)

    second = conv_dots(cols_h, w2, 0, rows, slab, False)
    summed = mine.reshape(rows, slab, ch) + second.reshape(rows, slab, ch)
    pairs = rows // 2
    for i in range(pairs):
        pool_tmp[i * slab : (i + 1) * slab, :] = summed[2 * i] + summed[2 * i + 1]
    for i in range(pairs):
        for f in range(frames):
            at = i * slab + f * cols
            pooled[0, f, i] = 0.25 * (
                pool_tmp[pl.ds(at, cols // 2, stride=2), :]
                + pool_tmp[pl.ds(at + 1, cols // 2, stride=2), :]
            )
    fill_columns(cols_a, four(act), same, True)
    back = conv_dots(cols_a, w1t, 0, rows, slab, True)
    total = (g_own + back).reshape(rows, frames, cols, ch)
    for r in range(rows):
        in_grad[0, :, r] = total[r]
    step_c(1)
    step_c(0)
    step_d(1)
    step_d(0)


def hand_out(*refs):
    sems = refs[8]
    copies = [pltpu.make_async_copy(refs[i], refs[4 + i], sems.at[i]) for i in (1, 2, 3, 0)]
    for copy in copies:
        copy.start()
    for copy in copies:
        copy.wait()


def local(n_tile, n_dp, clip_frames, segments, weight_first, weight_second, cotangent):
    _, frames, rows, cols, ch = clip_frames.shape
    slab = frames * cols
    taps = weight_first.shape[0]
    share = taps // n_tile
    n_z = n_tile // 2
    quarter = ch // n_dp
    part = up16(quarter)
    unit = math.gcd(share, quarter)
    per_quarter = quarter // unit

    def before(to, q):
        whole, rest = divmod(share // unit * to, ch // unit)
        return per_quarter * whole + min(max(rest - per_quarter * q, 0), per_quarter)

    n_unit = max(before(k + 1, q) - before(k, q) for k in range(n_tile) for q in range(n_dp))
    block = n_unit * (part // per_quarter)
    span = share + 2 * ch * (n_unit // per_quarter + 2)
    scale = 1.0 / math.sqrt(n_dp * n_tile * rows * slab)
    vmem = pl.BlockSpec(memory_space=pltpu.VMEM)
    cells = rows * slab
    lanes = (rows + 2) * slab
    sem = pltpu.SemaphoreType.DMA
    anywhere = pl.BlockSpec(memory_space=pltpu.HBM)
    shapes = (
        jax.ShapeDtypeStruct((1, frames, rows // 2, cols // 2, ch), F32),
        jax.ShapeDtypeStruct((1, frames, rows, cols, ch), F32),
        jax.ShapeDtypeStruct((share, ch), F32),
        jax.ShapeDtypeStruct((share, ch), F32),
    )
    held = [
        pltpu.with_memory_space_constraint(v, pltpu.HBM)
        for v in (segments, clip_frames, weight_first, weight_second, cotangent)
    ]
    results = pl.pallas_call(
        functools.partial(kernel, (n_tile, n_dp, share, quarter, part, unit, n_unit, scale)),
        out_shape=shapes,
        in_specs=[pl.BlockSpec(memory_space=pltpu.SMEM)] + [anywhere] * 4,
        out_specs=(vmem,) * 4,
        scratch_shapes=[
            pltpu.VMEM((rows, frames, cols, ch), BF16),
            pltpu.VMEM((taps, ch), BF16),
            pltpu.VMEM((taps, ch), BF16),
            pltpu.VMEM((rows // 2, frames, cols // 2, ch), BF16),
            pltpu.VMEM(((rows // 2 + 2) * slab, ch), F32),
            sem((2 + rows + rows // 2,)),
            pltpu.VMEM((2, 2 * slab + slab // 2, ch), BF16),
            pltpu.VMEM((2, 2 * slab + slab // 2, ch), BF16),
            pltpu.VMEM(((rows + 4) * slab, 9 * ch), BF16),
            pltpu.VMEM(((rows + 2) * slab, 9 * ch), BF16),
            pltpu.VMEM(((rows + 4) * slab, 9 * ch), BF16),
            pltpu.VMEM(((rows + 2) * slab, 9 * ch), BF16),
            pltpu.VMEM((taps, ch), BF16),
            pltpu.VMEM((taps, ch), BF16),
            pltpu.VMEM((cells // 2, ch), F32),
            pltpu.VMEM((lanes, ch), F32),
            pltpu.VMEM((lanes, ch), F32),
            pltpu.VMEM((n_dp, cells - 2 * slab, ch), BF16),
            pltpu.VMEM((n_dp, 9, 8, 2 * slab), F32),
            pltpu.VMEM((cells // 4, ch), BF16),
            pltpu.VMEM((n_dp, cells // ch * part + cells // 4 + 16, ch), BF16),
            pltpu.VMEM((n_dp, cells // ch * part + cells // 4 + 16, ch), BF16),
            pltpu.VMEM((n_dp, (cells // ch + 2) * part, ch), BF16),
            pltpu.VMEM((n_dp, (cells // ch + 2) * part, ch), BF16),
            pltpu.VMEM((n_dp, 2 * slab, ch), BF16),
            pltpu.VMEM((n_dp, cells, ch), BF16),
            pltpu.VMEM((2, n_dp, taps // ch * part, cells), BF16),
            pltpu.VMEM((2, taps // ch * part, ch), F32),
            pltpu.VMEM((2, n_z, block, ch), F32),
            pltpu.VMEM((2, block, ch), F32),
            pltpu.VMEM((2, n_z - 1, block, ch), BF16),
            pltpu.VMEM((2, n_z - 1, block, ch), BF16),
            pltpu.VMEM((2, n_dp, block, ch), BF16),
            pltpu.VMEM((2, span, ch), F32),
            sem((2,)), sem((2,)),
            sem((n_dp - 1,)), sem((n_dp - 1,)),
            sem((n_dp - 1,)), sem((n_dp - 1,)),
            sem((n_dp - 1,)), sem((n_dp - 1,)),
            sem((n_dp - 1,)), sem((n_dp - 1,)),
            sem((2, n_z)), sem((2, n_z)),
            sem((2, n_z - 1)), sem((2, n_z - 1)),
            sem((2, n_dp - 1)), sem((2, n_dp - 1)),
        ],
        compiler_params=pltpu.CompilerParams(
            collective_id=0, has_side_effects=True, vmem_limit_bytes=50 * 1024 * 1024
        ),
    )(*held)
    return tuple(
        pl.pallas_call(
            hand_out,
            out_shape=shapes,
            in_specs=[pl.BlockSpec(memory_space=pl.ANY)] * 4,
            out_specs=(pl.BlockSpec(memory_space=pl.ANY),) * 4,
            scratch_shapes=[sem((4,))],
            compiler_params=pltpu.CompilerParams(vmem_limit_bytes=4 * 1024 * 1024),
        )(*results)
    )


def solution(mesh):
    return jax.shard_map(
        functools.partial(local, mesh.shape["tile"], mesh.shape["dp"]),
        mesh=mesh,
        in_specs=(
            P("dp", None, "tile", None, None),
            P("dp", None),
            P(),
            P(),
            P("dp", None, "tile", None, None),
        ),
        out_specs=(
            P("dp", None, "tile", None, None),
            P("dp", None, "tile", None, None),
            P("tile", None),
            P("tile", None),
        ),
        check_vma=False,
    )
```
